256 devices in a mesh: ep: 64 (over z, x, core), tp: 4 (over y).
Axes of the slice: x: 4, y: 4, z: 8, core: 2. Of those that a mesh axis runs over, the one named last changes fastest.
Arguments:
- features: bfloat16 [16384, 1024], P('ep'), may hold values from -6 to 6
- cotangent: bfloat16 [16384, 2048], P('ep'), may hold values from -6 to 6
- expert_ids: int32 [16384, 2], P('ep'), may hold values from 0 to 7, all different within a row; in each aligned block of 32 rows (0 to 31, 32 to 63, ...) at most 12 rows name the same one
- gate_levels: int32 [16384, 2], P('ep'), may hold values from 1 to 15
- w_in: bfloat16 [64, 1024, 512], P('ep', None, 'tp'), may hold values from -0.1875 to 0.1875
- w_out: bfloat16 [64, 512, 2048], P('ep', 'tp'), may hold values from -0.09375 to 0.09375
Outputs:
- grad_in: bfloat16 [16384, 1024], P('ep', 'tp')
- grad_w_in: bfloat16 [64, 1024, 512], P('ep', None, 'tp')
- grad_w_out: bfloat16 [64, 512, 2048], P('ep', 'tp')
The draws below stay inside these ranges and needn't reach their ends.
Inputs may be any that keep to these rules, and one draw needn't show every extreme that they name: `expert_ids`: each row names two different experts. In each aligned block of 32 rows no expert is named by more than 12 rows, and some expert reaches 12 rows in some block.
All inputs are finite; a program needn't handle non-finite values.
Results may differ from the reference program's by a relative error of at most 0.0065.
Values may be sent and summed in bfloat16 or wider, within the bound.
A program may use at most 128 MiB of HBM per device.

```python
import math
import jax
import jax.numpy as jnp
import numpy as np
from jax import lax

DIN = 1024
H = 4096
DOUT = 2048
E = 8
R = 8
SUB = 32
CAP = 12
TOKENS = 16384
N_EP = 64


def with_ends(drawn, stream_key, smallest, largest):
    dims = drawn.shape
    place = [jax.random.randint(jax.random.fold_in(stream_key, axis), (), 0, dims[axis]) for axis in range(len(dims))]
    drawn = drawn.at[tuple(place)].set(smallest)
    longest = dims.index(max(dims))
    place[longest] = (place[longest] + 1) % dims[longest]
    return drawn.at[tuple(place)].set(largest)


def block_levels(own_key, shape, split, smallest, high):
    level, own = 1.0, jax.random.fold_in(own_key, 6)
    for axis_at, blocks in split:
        heights = jnp.exp(jax.random.uniform(jax.random.fold_in(own, axis_at), (blocks,), jnp.float32, smallest / len(split), high / len(split)))
        level = level * jnp.repeat(heights, shape[axis_at] // blocks).reshape([-1 if axis == axis_at else 1 for axis in range(len(shape))])
    return level


def assign_block(own_key, own, number, rows, count, top, reach, lean):
    sequence = jax.random.permutation(own_key, count)
    heavy_load, usual = shares(count, rows * top, reach, lean, True), shares(count, rows * top, reach, lean, False)
    places = jnp.arange(count)

    def named(sizes, rotation):
        used = int((sizes > 0).sum())
        fixed = max(1, used // 4)
        passed = fixed + (places - fixed + rotation * (used - fixed)) % max(1, count - fixed)
        return jnp.zeros((count,), jnp.int32).at[sequence[jnp.where(places < fixed, places, passed)]].set(jnp.asarray(sizes, jnp.int32))

    sizes = jnp.where(number % 4 == 0, named(heavy_load, number // 4), named(usual, number - number // 4 - 1))
    mixed = jax.random.permutation(jax.random.fold_in(own, 3), count)
    donor, receiver = mixed[0:count // 2 * 2:2], mixed[1:count // 2 * 2:2]
    room = jnp.minimum(sizes[donor] - 1, reach - sizes[receiver]) // 2
    room = jnp.where((donor == sequence[0]) | (receiver == sequence[0]) | (sizes[receiver] == 0), 0, jnp.maximum(room, 0))
    passed = jax.random.randint(jax.random.fold_in(own, 4), (count // 2,), 0, 1 << 20) % (room + 1)
    sizes = sizes.at[donor].add(-passed).at[receiver].add(passed)
    items = jnp.searchsorted(jnp.cumsum(sizes), jnp.arange(rows * top), side="right").astype(jnp.int32)
    listing = items.reshape(top, rows).T
    listing = listing[jax.random.permutation(jax.random.fold_in(own, 1), rows)]
    rotation = jax.random.randint(jax.random.fold_in(own, 2), (rows, 1), 0, top)
    return jnp.take_along_axis(listing, (jnp.arange(top)[None, :] + rotation) % top, axis=1)


def shares(number_of, total, limit, slope, full):
    loads = [(1 << 20) // math.isqrt(rank ** slope) + 1 for rank in range(1, number_of + 1)]
    largest = limit if full else min(limit, max(-(-total // number_of), total * loads[0] // sum(loads)))
    least = 1 if total - largest >= number_of - 1 else 0
    counts, rest = [largest] + [least] * (number_of - 1), total - largest - least * (number_of - 1)
    while rest > 0:
        candidates = [i for i in range(1, number_of) if counts[i] < largest] or [i for i in range(1, number_of) if counts[i] < limit]
        whole, left = sum([loads[i] for i in candidates]), rest
        for i in candidates:
            addition = min(limit - counts[i], max(1, left * loads[i] // whole), rest)
            counts[i] = counts[i] + addition
            rest = rest - addition
    return np.array(counts)


def noise(key, extent, scale, limit, pieces=(), kind=jnp.bfloat16):
    entries = scale * jax.random.normal(key, extent, jnp.float32)
    if pieces:
        entries = entries * block_levels(key, extent, pieces, -0.22, 0.18)
    return jnp.clip(entries, -limit, limit).astype(kind)


def setup_inputs(seed: int = 0) -> dict:
    seeds = jax.random.split(jax.random.key(seed), 7)
    features = noise(seeds[0], (TOKENS, DIN), 1.0, 6.0, ((0, 64),))
    cotangent = noise(seeds[1], (TOKENS, DOUT), 1.0, 6.0, ((0, 64),))
    expert_ids_keys = jax.random.split(jax.random.fold_in(seeds[2], 1), TOKENS // SUB)
    expert_ids_turns = jax.random.permutation(jax.random.fold_in(seeds[2], 3), TOKENS // SUB)
    expert_ids = jax.vmap(lambda own, number: assign_block(jax.random.fold_in(seeds[2], 2), own, number, SUB, E, 2, CAP, 2))(expert_ids_keys, expert_ids_turns).reshape((TOKENS, 2))
    gate_levels = with_ends(jax.random.randint(seeds[3], (TOKENS, 2), 1, 16), jax.random.fold_in(seeds[3], 1), 1, 15).astype(jnp.int32)
    w_in = noise(seeds[4], (N_EP, DIN, H // R), DIN ** -0.5, 0.1875, ((0, 64), (2, 4)))
    w_out = noise(seeds[5], (N_EP, H // R, DOUT), H ** -0.5, 0.09375, ((0, 64), (1, 4)))
    return dict(features=features, cotangent=cotangent, expert_ids=expert_ids, gate_levels=gate_levels, w_in=w_in, w_out=w_out)


def reference(features, cotangent, expert_ids, gate_levels, w_in, w_out):
    block_count = TOKENS // SUB
    flattened = expert_ids.reshape(block_count, 2 * SUB)
    one_hot = (flattened[:, :, None] == jnp.arange(E, dtype=jnp.int32)[None, None, :]).astype(jnp.int32)
    earlier = jnp.cumsum(one_hot, axis=1) - one_hot
    within = lax.optimization_barrier(jnp.sum(one_hot * earlier, axis=2)).astype(jnp.int32)
    block_ids = jnp.arange(block_count, dtype=jnp.int32)[:, None]
    buffer_rows = block_count * CAP
    pair_count = 2 * TOKENS
    pair_range = jnp.arange(pair_count, dtype=jnp.int32)
    gate_values = gate_levels.reshape(-1).astype(jnp.float32) / 16.0
    grad_scale = 1.0 / math.sqrt(2.0 * TOKENS / E)
    hidden_part = H // R
    input_total = jnp.zeros((TOKENS, DIN), jnp.float32)
    grads_first = []
    grads_second = []
    for expert in range(E):
        target = jnp.where(flattened == expert, block_ids * CAP + within, buffer_rows).reshape(-1).astype(jnp.int32)
        owner = jnp.full((buffer_rows,), pair_count, jnp.int32).at[target].set(pair_range, mode='drop')
        filled = owner < pair_count
        pair_ids = jnp.minimum(owner, pair_count - 1).astype(jnp.int32)
        token_ids = (pair_ids // 2).astype(jnp.int32)
        rows_x = features[token_ids] * filled.astype(jnp.bfloat16)[:, None]
        slot_gates = jnp.where(filled, gate_values[pair_ids], jnp.float32(0.0))
        rows_dy = (cotangent[token_ids].astype(jnp.float32) * slot_gates[:, None]).astype(jnp.bfloat16)
        weight_in = jnp.concatenate([w_in[replica * E + expert] for replica in range(R)], axis=1)
        weight_out = jnp.concatenate([w_out[replica * E + expert] for replica in range(R)], axis=0)
        pre = jnp.dot(rows_x, weight_in, preferred_element_type=jnp.float32)
        activated, gelu_back = jax.vjp(jax.nn.gelu, pre)
        act_rows = activated.astype(jnp.bfloat16)
        back_act = jnp.dot(rows_dy, weight_out.T, preferred_element_type=jnp.float32)
        back_pre = gelu_back(back_act)[0].astype(jnp.bfloat16)
        second = jnp.dot(act_rows.T, rows_dy, preferred_element_type=jnp.float32)
        grads_second.append((second * grad_scale).astype(jnp.bfloat16))
        first = jnp.dot(rows_x.T, back_pre, preferred_element_type=jnp.float32)
        grads_first.append((first * grad_scale).astype(jnp.bfloat16))
        slot_input = jnp.dot(back_pre, weight_in.T, preferred_element_type=jnp.float32).astype(jnp.bfloat16)
        input_total = input_total.at[token_ids].add(slot_input.astype(jnp.float32) * filled.astype(jnp.float32)[:, None])
    grad_in = input_total.astype(jnp.bfloat16)
    grad_w_in = jnp.stack([grads_first[device % E][:, device // E * hidden_part:(device // E + 1) * hidden_part] for device in range(N_EP)])
    grad_w_out = jnp.stack([grads_second[device % E][device // E * hidden_part:(device // E + 1) * hidden_part, :] for device in range(N_EP)])
    return (grad_in, grad_w_in, grad_w_out)
```

```python
import functools
import math

import jax
import jax.numpy as jnp
from jax import lax
from jax.experimental import pallas as pl
from jax.experimental.pallas import tpu as pltpu
from jax.sharding import PartitionSpec as P

MESH = pl.DeviceIdType.MESH
E = 8
NZ, NX, NC, NY = 8, 4, 2, 4
SLOTS = 96
ROWS = E * SLOTS
TOK = 256
DIN = 1024
DOUT = 2048
SPAN = 128
QY = DOUT // NY
QX = DIN // NY
TILE = 256
NT = ROWS // TILE
F32 = jnp.float32
BF16 = jnp.bfloat16


def dot_nn(a, b):
    return lax.dot_general(a, b, (((1,), (0,)), ((), ())), preferred_element_type=F32)


def dot_nt(a, b):
    return lax.dot_general(a, b, (((1,), (1,)), ((), ())), preferred_element_type=F32)


def dot_tn(a, b):
    return lax.dot_general(a, b, (((0,), (0,)), ((), ())), preferred_element_type=F32)


def gelu_parts(v):
    k = math.sqrt(2.0 / math.pi)
    vv = v * v
    t = jnp.tanh(k * (v + 0.044715 * (v * vv)))
    half = 0.5 * (1.0 + t)
    act = v * half
    slope = half + 0.5 * v * (1.0 - t * t) * (k * (1.0 + 3.0 * 0.044715 * vv))
    return act, slope


def kernel(
    grad_scale,
    x_ref, dy_ref, ids_ref, gate_ref, w1_ref, w2_ref,
    gin_ref, g1_ref, g2_ref,
    p_ref, pg_ref, packx, packy, xr, dyr, w1b, w2b, actt, bpret,
    own, sbuf, rbuf, partown, parts, partr, retb, retr,
    ag_s, ag_r, rs_s, rs_r, dx_s, dx_r, dc_s, dc_r, fw_s, fw_r, pt_s, pt_r, rt_s, rt_r,
):
    ep = lax.axis_index("ep")
    y = lax.axis_index("tp")
    z = ep // E
    me = lax.rem(ep, E)
    x = me // NC
    c = lax.rem(me, NC)
    right = (lax.rem(z + 1, NZ) * E + me, y)
    left = (lax.rem(z + NZ - 1, NZ) * E + me, y)

    def plane(e):
        return (z * E + e, y)

    def yrank(k):
        return lax.rem(y + k, NY)

    def remote(src, dst, ss, rs, dev):
        return pltpu.make_async_remote_copy(
            src_ref=src, dst_ref=dst, send_sem=ss, recv_sem=rs, device_id=dev, device_id_type=MESH
        )

    bar = pltpu.get_barrier_semaphore()
    for dev in (left, right):
        pl.semaphore_signal(bar, inc=1, device_id=dev, device_id_type=MESH)
    for k in range(1, E):
        pl.semaphore_signal(bar, inc=1, device_id=plane(lax.rem(me + k, E)), device_id_type=MESH)
    for k in range(1, NY):
        pl.semaphore_signal(bar, inc=1, device_id=(ep, yrank(k)), device_id_type=MESH)
    pl.semaphore_wait(bar, 2 + E - 1 + NY - 1)

    def wchunk(slot, ch):
        return w1b.at[slot] if ch == 0 else w2b.at[slot, ch - 1]

    def ag(direction, step, ch):
        if step == 0:
            src_slot = 0
        else:
            src_slot = 2 * step - 1 + direction
        dst_slot = 7 if step == 3 else 2 * step + 1 + direction
        src, dst = wchunk(src_slot, ch), wchunk(dst_slot, ch)
        if step == 3:
            half = pl.ds(direction * (SPAN // 2), SPAN // 2)
            src, dst = src.at[half], dst.at[half]
        return remote(src, dst, ag_s.at[direction, step, ch], ag_r.at[direction, step, ch],
                      left if direction == 0 else right)

    order = (1, 2, 0)
    for h in range(2):
        w2b[0, h] = w2_ref[0, :, h * DIN:(h + 1) * DIN]
        for direction in range(2):
            ag(direction, 0, 1 + h).start()
    w1b[0] = w1_ref[0].astype(F32).T.astype(BF16)
    for direction in range(2):
        ag(direction, 0, 0).start()

    def ag_pass(step):
        for ch in order:
            for direction in range(2):
                ag(direction, step - 1, ch).wait_recv()
                if step <= 3:
                    ag(direction, step, ch).start()

    lanes = lax.broadcasted_iota(jnp.int32, (TOK, 128), 1)
    first = ids_ref[:, 0:1] == lanes
    second = ids_ref[:, 1:2] == lanes
    named = jnp.where(first | second, 1.0, 0.0)
    gates = gate_ref[...].astype(F32) * (1.0 / 16.0)
    gate_of = jnp.where(first, gates[:, 0:1], 0.0) + jnp.where(second, gates[:, 1:2], 0.0)
    named_t = named.T[:16]
    gate_t = gate_of.T[:16].astype(BF16)
    before = (
        lax.broadcasted_iota(jnp.int32, (TOK, TOK), 0) < lax.broadcasted_iota(jnp.int32, (TOK, TOK), 1)
    ).astype(F32).astype(BF16)
    rank = dot_nn(named_t.astype(BF16), before)
    rank = jnp.where(named_t > 0.5, rank, -1.0).astype(BF16)
    for e in range(E):
        slot = lax.broadcasted_iota(jnp.int32, (SLOTS, TOK), 0).astype(F32)
        hit = jnp.broadcast_to(rank[e:e + 1].astype(F32), (SLOTS, TOK)) == slot
        p_ref[e * SLOTS:(e + 1) * SLOTS] = jnp.where(hit, 1.0, 0.0).astype(BF16)
        pg_ref[e * SLOTS:(e + 1) * SLOTS] = jnp.where(
            hit, jnp.broadcast_to(gate_t[e:e + 1].astype(F32), (SLOTS, TOK)), 0.0
        ).astype(BF16)

    def rows_of(e):
        return pl.ds(pl.multiple_of(e * SLOTS, 32), SLOTS)

    mine = rows_of(me)
    sib = me + 1 - 2 * c

    def cot_send(e):
        return remote(packy.at[y, rows_of(e)], dyr.at[y, mine], dc_s.at[e], dc_r.at[me], plane(e))

    def cot_recv(e):
        return remote(packy.at[y, rows_of(e)], dyr.at[y, rows_of(e)], dc_s.at[e], dc_r.at[e], plane(e))

    def cot_sib(target, source):
        return remote(packy.at[:, rows_of(target)], dyr.at[:, rows_of(source)], dc_s.at[target], dc_r.at[source],
                      plane(target))

    def pack_cot(e):
        rows = rows_of(e)
        for q in range(NY):
            packy[q, rows] = dot_nn(pg_ref[rows], dy_ref[:, q * QY:(q + 1) * QY]).astype(BF16)

    far = E - NC

    def other(k):
        return lax.rem(x * NC + NC + k, E)

    @pl.loop(0, far)
    def _(k):
        e = other(k)
        pack_cot(e)
        cot_send(e).start()

    def feat_send(e):
        return remote(packx.at[rows_of(e)], xr.at[mine], dx_s.at[e], dx_r.at[me], plane(e))

    def feat_recv(e):
        return remote(packx.at[rows_of(e)], xr.at[rows_of(e)], dx_s.at[e], dx_r.at[e], plane(e))

    def pack_feat(e):
        rows = rows_of(e)
        packx[rows] = dot_nn(p_ref[rows], x_ref[...]).astype(BF16)

    @pl.loop(0, far)
    def _(k):
        e = other(k)
        pack_feat(e)
        feat_send(e).start()

    pack_cot(sib)
    cot_sib(sib, me).start()
    pack_feat(sib)
    feat_send(sib).start()
    for q in range(NY):
        dyr[q, mine] = dot_nn(pg_ref[mine], dy_ref[:, q * QY:(q + 1) * QY]).astype(BF16)
    xr[mine] = dot_nn(p_ref[mine], x_ref[...]).astype(BF16)

    def chip_rows(k):
        return pl.ds(pl.multiple_of(lax.rem(x + k, NX) * NC * SLOTS, 64), NC * SLOTS)

    def fw_send(k, j):
        part = dyr.at[y, chip_rows(k)]
        return remote(part, part, fw_s.at[k - 1, j - 1], fw_r.at[k - 1, j - 1], (ep, yrank(j)))

    def fw_recv(k, j):
        part = dyr.at[yrank(NY - j), chip_rows(k)]
        return remote(part, part, fw_s.at[k - 1, j - 1], fw_r.at[k - 1, j - 1], (ep, yrank(j)))

    for k in (1, 3, 2):
        for cc in range(NC):
            cot_recv(lax.rem(x + k, NX) * NC + cc).wait_recv()
        for j in (1, 3, 2):
            fw_send(k, j).start()

    ag_pass(1)

    def forward(s0, n):
        w1 = w1b[s0:s0 + n].reshape(n * SPAN, DIN)
        w2 = [w2b[s0:s0 + n, h].reshape(n * SPAN, DIN) for h in range(2)]

        @pl.loop(0, NT)
        def _(t):
            rows = pl.ds(pl.multiple_of(t * TILE, TILE), TILE)
            pre = dot_nt(w1, xr[rows])
            back = dot_nt(w2[0][:, :QY], dyr[0, rows])
            for q in range(1, NY):
                back += dot_nt(w2[q // 2][:, (q % 2) * QY:(q % 2 + 1) * QY], dyr[q, rows])
            act, slope = gelu_parts(pre)
            actt[t, s0:s0 + n] = act.astype(BF16).reshape(n, SPAN, TILE)
            bpret[t, s0:s0 + n] = (back * slope).astype(BF16).reshape(n, SPAN, TILE)

    def weight_grads(s0, n):
        def lhs(buf, t):
            return buf[t, s0:s0 + n].reshape(n * SPAN, TILE)

        for half in range(2):
            cols = slice(half * 512, (half + 1) * 512)
            total = dot_nn(lhs(bpret, 0), xr[0:TILE, cols])
            for t in range(1, NT):
                total += dot_nn(lhs(bpret, t), xr[t * TILE:(t + 1) * TILE, cols])
            own[0:n, 0, :, cols] = total.reshape(n, SPAN, 512)
        for q in range(NY):
            total = dot_nn(lhs(actt, 0), dyr[q, 0:TILE])
            for t in range(1, NT):
                total += dot_nn(lhs(actt, t), dyr[q, t * TILE:(t + 1) * TILE])
            own[0:n, 1 + q // 2, :, (q % 2) * QY:(q % 2 + 1) * QY] = total.reshape(n, SPAN, QY)

    @pl.loop(1, E)
    def _(k):
        feat_recv(lax.rem(me + k, E)).wait_recv()

    ag_pass(2)
    cot_sib(sib, sib).wait_recv()
    for k in (1, 3, 2):
        for j in (1, 3, 2):
            fw_recv(k, j).wait_recv()
    forward(0, 1)
    forward(1, 2)
    forward(3, 2)
    ag_pass(3)
    forward(5, 2)

    def rs(direction, step, ch):
        src, dst = sbuf.at[direction, step, ch], rbuf.at[direction, step, ch]
        if step == 0:
            half = pl.ds(direction * (SPAN // 2), SPAN // 2)
            src, dst = src.at[half], dst.at[half]
        return remote(src, dst, rs_s.at[direction, step, ch], rs_r.at[direction, step, ch],
                      right if direction == 0 else left)

    ag_pass(4)
    forward(7, 1)
    weight_grads(7, 1)
    for ch in order:
        for direction in range(2):
            half = slice(direction * (SPAN // 2), (direction + 1) * (SPAN // 2))
            sbuf[direction, 0, ch, half] = own[0, ch, half].astype(BF16)
            rs(direction, 0, ch).start()

    def rs_pass(step):
        for ch in order:
            for direction in range(2):
                rs(direction, step - 1, ch).wait_recv()
                if step == 1:
                    got = slice(direction * (SPAN // 2), (direction + 1) * (SPAN // 2))
                    rest = slice((1 - direction) * (SPAN // 2), (2 - direction) * (SPAN // 2))
                    sbuf[direction, step, ch, rest] = own[direction, ch, rest].astype(BF16)
                else:
                    got = slice(0, SPAN)
                sbuf[direction, step, ch, got] = (
                    own[direction, ch, got] + rbuf[direction, step - 1, ch, got].astype(F32)
                ).astype(BF16)
                rs(direction, step, ch).start()

    weight_grads(5, 2)
    rs_pass(1)
    weight_grads(3, 2)

    def part_send(j):
        return remote(parts.at[j - 1], partr.at[j - 1], pt_s.at[j - 1], pt_r.at[j - 1], (ep, yrank(j)))

    def part_dot(t, q):
        cols = pl.ds(pl.multiple_of(q * QX, QX), QX)
        return dot_tn(bpret[t].reshape(NZ * SPAN, TILE), w1b[:, :, cols].reshape(NZ * SPAN, QX))

    for j in (2, 1, 3):
        @pl.loop(0, NT)
        def _(t):
            rows = pl.ds(pl.multiple_of(t * TILE, TILE), TILE)
            parts[j - 1, rows] = part_dot(t, yrank(j)).astype(BF16)
        part_send(j).start()

    @pl.loop(0, NT)
    def _(t):
        partown[pl.ds(pl.multiple_of(t * TILE, TILE), TILE)] = part_dot(t, y)

    rs_pass(2)
    weight_grads(1, 2)

    def ret_send(e):
        return remote(retb.at[rows_of(e)], retr.at[mine], rt_s.at[e], rt_r.at[me], plane(e))

    def ret_recv(e):
        return remote(retb.at[rows_of(e)], retr.at[rows_of(e)], rt_s.at[e], rt_r.at[e], plane(e))

    for j in (1, 3, 2):
        part_send(j).wait_recv()
    retb[...] = (
        partown[...] + partr[0].astype(F32) + partr[1].astype(F32) + partr[2].astype(F32)
    ).astype(BF16)

    @pl.loop(1, E)
    def _(k):
        ret_send(lax.rem(me + k, E)).start()

    retr[mine] = retb[mine]
    rs_pass(3)
    weight_grads(0, 1)

    @pl.loop(1, E)
    def _(k):
        ret_recv(lax.rem(me + k, E)).wait_recv()

    gin_ref[...] = dot_tn(p_ref[...], retr[...]).astype(BF16)

    for ch in order:
        for direction in range(2):
            rs(direction, 3, ch).wait_recv()
        total = (own[0, ch] + rbuf[0, 3, ch].astype(F32) + rbuf[1, 3, ch].astype(F32)) * grad_scale
        if ch == 0:
            g1_ref[0] = total.T.astype(BF16)
        else:
            g2_ref[0, :, (ch - 1) * DIN:ch * DIN] = total.astype(BF16)

    for step in range(4):
        for ch in order:
            for direction in range(2):
                ag(direction, step, ch).wait_send()
                rs(direction, step, ch).wait_send()

    @pl.loop(0, far)
    def _(k):
        cot_send(other(k)).wait_send()

    cot_sib(sib, me).wait_send()
    for k in range(1, NX):
        for j in range(1, NY):
            fw_send(k, j).wait_send()
    for j in range(1, NY):
        part_send(j).wait_send()

    @pl.loop(1, E)
    def _(k):
        feat_send(lax.rem(me + k, E)).wait_send()
        ret_send(lax.rem(me + k, E)).wait_send()


def shards(features, cotangent, expert_ids, gate_levels, w_in, w_out):
    tokens = features.shape[0] * lax.axis_size("ep")
    grad_scale = 1.0 / math.sqrt(2.0 * tokens / E)
    vm = pl.BlockSpec(memory_space=pltpu.VMEM)
    dma = pltpu.SemaphoreType.DMA


    return pl.pallas_call(
        functools.partial(kernel, grad_scale),
        out_shape=(
            jax.ShapeDtypeStruct((TOK, QX), BF16),
            jax.ShapeDtypeStruct((1, DIN, SPAN), BF16),
            jax.ShapeDtypeStruct((1, SPAN, DOUT), BF16),
        ),
        in_specs=[vm] * 6,
        out_specs=(vm, vm, vm),
        scratch_shapes=[
            pltpu.VMEM((ROWS, TOK), BF16),
            pltpu.VMEM((ROWS, TOK), BF16),
            pltpu.VMEM((ROWS, DIN), BF16),
            pltpu.VMEM((NY, ROWS, QY), BF16),
            pltpu.VMEM((ROWS, DIN), BF16),
            pltpu.VMEM((NY, ROWS, QY), BF16),
            pltpu.VMEM((NZ, SPAN, DIN), BF16),
            pltpu.VMEM((NZ, 2, SPAN, DIN), BF16),
            pltpu.VMEM((NT, NZ, SPAN, TILE), BF16),
            pltpu.VMEM((NT, NZ, SPAN, TILE), BF16),
            pltpu.VMEM((2, 3, SPAN, DIN), F32),
            pltpu.VMEM((2, 4, 3, SPAN, DIN), BF16),
            pltpu.VMEM((2, 4, 3, SPAN, DIN), BF16),
            pltpu.VMEM((ROWS, QX), F32),
            pltpu.VMEM((NY - 1, ROWS, QX), BF16),
            pltpu.VMEM((NY - 1, ROWS, QX), BF16),
            pltpu.VMEM((ROWS, QX), BF16),
            pltpu.VMEM((ROWS, QX), BF16),
            dma((2, 4, 3)), dma((2, 4, 3)),
            dma((2, 4, 3)), dma((2, 4, 3)),
            dma((E,)), dma((E,)),
            dma((E,)), dma((E,)),
            dma((NX - 1, NY - 1)), dma((NX - 1, NY - 1)),
            dma((NY - 1,)), dma((NY - 1,)),
            dma((E,)), dma((E,)),
        ],
        compiler_params=pltpu.CompilerParams(
            collective_id=0, has_side_effects=True, vmem_limit_bytes=60 * 1024 * 1024
        ),
        cost_estimate=pl.CostEstimate(flops=11_300_000_000, bytes_accessed=5_000_000, transcendentals=0),
        name="moe_backward",
    )(features, cotangent, expert_ids, gate_levels, w_in, w_out)


def solution(mesh):
    return jax.shard_map(
        shards,
        mesh=mesh,
        in_specs=(
            P("ep", None),
            P("ep", None),
            P("ep", None),
            P("ep", None),
            P("ep", None, "tp"),
            P("ep", "tp", None),
        ),
        out_specs=(P("ep", "tp"), P("ep", None, "tp"), P("ep", "tp", None)),
        check_vma=False,
    )
```

```python
import functools
import math

import jax
import jax.numpy as jnp
from jax import lax
from jax.experimental import pallas as pl
from jax.experimental.pallas import tpu as pltpu
from jax.sharding import PartitionSpec as P

MESH = pl.DeviceIdType.MESH
E = 8
NZ, NX, NC, NY = 8, 4, 2, 4
TOK = 256
QT = TOK // NY
DIN = 1024
DOUT = 2048
SPAN = 128
QX = DIN // NY
SL = 48
G = NX * SL
CB = 512
WB = DIN + CB
WA = DOUT - CB
HALF = 2 * SPAN
ROWS = NZ * G
F32 = jnp.float32
BF16 = jnp.bfloat16


def dot_nn(a, b):
    return lax.dot_general(a, b, (((1,), (0,)), ((), ())), preferred_element_type=F32)


def dot_nt(a, b):
    return lax.dot_general(a, b, (((1,), (1,)), ((), ())), preferred_element_type=F32)


def dot_tn(a, b):
    return lax.dot_general(a, b, (((0,), (0,)), ((), ())), preferred_element_type=F32)


def gelu_parts(v):
    k = math.sqrt(2.0 / math.pi)
    vv = v * v
    t = jnp.tanh(k * (v + 0.044715 * (v * vv)))
    half = 0.5 * (1.0 + t)
    act = v * half
    slope = half + 0.5 * v * (1.0 - t * t) * (k * (1.0 + 3.0 * 0.044715 * vv))
    return act, slope


def kernel(
    grad_scale,
    x_ref, dy_ref, ids_ref, gate_ref, w1_ref, w2_ref,
    gin_ref, g1_ref, g2_ref,
    rawb, rawa, meta, p_ref, pg_ref, packa, packb, rowsa, rowsb,
    w1v, w1b, w2b, actb, bpb, pown, sbuf, rbuf, gown, gsend, grecv,
    retb, retr, sibs, sibr, giny, gout, gv1, gv2,
    ld, st, zb_s, zb_r, zm_s, zm_r, sb_s, sb_r, sm_s, sm_r, sa_s, sa_r,
    xb_s, xb_r, xa_s, xa_r, za_s, za_r, wy_s, wy_r, rs_s, rs_r, gy_s, gy_r,
    rt_s, rt_r, s2_s, s2_r, yo_s, yo_r,
):
    ep = lax.axis_index("ep")
    y = lax.axis_index("tp")
    z = ep // E
    me = lax.rem(ep, E)
    x = me // NC
    c = lax.rem(me, NC)
    right = (lax.rem(z + 1, NZ) * E + me, y)
    left = (lax.rem(z + NZ - 1, NZ) * E + me, y)
    sibling = (z * E + me + 1 - 2 * c, y)

    def xrank(k):
        return lax.rem(x + k, NX)

    def xdev(k):
        return (z * E + xrank(k) * NC + c, y)

    def yrank(k):
        return lax.rem(y + k, NY)

    def remote(src, dst, ss, rs, dev):
        return pltpu.make_async_remote_copy(
            src_ref=src, dst_ref=dst, send_sem=ss, recv_sem=rs, device_id=dev, device_id_type=MESH
        )

    quarter = pl.ds(pl.multiple_of(y * QT, QT), QT)
    loads = [
        pltpu.make_async_copy(x_ref.at[quarter], rawb.at[0, c, :, pl.ds(0, DIN)], ld.at[0]),
        pltpu.make_async_copy(dy_ref.at[quarter, pl.ds(0, CB)], rawb.at[0, c, :, pl.ds(DIN, CB)], ld.at[1]),
        pltpu.make_async_copy(dy_ref.at[quarter, pl.ds(CB, WA)], rawa.at[c], ld.at[2]),
        pltpu.make_async_copy(w2_ref.at[0], w2b.at[0], ld.at[3]),
        pltpu.make_async_copy(w1_ref.at[0], w1v, ld.at[4]),
    ]
    for load in loads:
        load.start()

    bar = pltpu.get_barrier_semaphore()
    partners = [left, right, sibling]
    partners += [xdev(k) for k in range(1, NX)] + [(ep, yrank(k)) for k in range(1, NY)]
    for dev in partners:
        pl.semaphore_signal(bar, inc=1, device_id=dev, device_id_type=MESH)
    pl.semaphore_wait(bar, len(partners))

    def slots(direction, step):
        src = 0 if step == 0 else 2 * step - 1 + direction
        return src, (7 if step == 3 else 2 * step + 1 + direction)

    def toward(direction):
        return left if direction == 0 else right

    def raw_ring(direction, step):
        s, d = slots(direction, step)
        src, dst = rawb.at[s, c], rawb.at[d, c]
        if step == 3:
            half = pl.ds(direction * (QT // 2), QT // 2)
            src, dst = src.at[half], dst.at[half]
        return remote(src, dst, zb_s.at[direction, step], zb_r.at[direction, step], toward(direction))

    def meta_ring(direction, step):
        s, d = slots(direction, step)
        return remote(meta.at[s, c], meta.at[d, c], zm_s.at[direction, step], zm_r.at[direction, step],
                      toward(direction))

    def has_meta(direction, step):
        return step < 3 or direction == 0

    def row_ring(direction, step, h):
        s, d = slots(direction, step)
        half = pl.ds(h * (G // 2), G // 2)
        return remote(rowsa.at[s, half], rowsa.at[d, half], za_s.at[direction, step, h], za_r.at[direction, step, h],
                      toward(direction))

    def row_halves(direction, step):
        return (direction,) if step == 3 else (0, 1)

    def raw_sib(slot, core):
        return remote(rawb.at[slot, core], rawb.at[slot, core], sb_s.at[slot], sb_r.at[slot], sibling)

    def meta_sib(slot, core):
        return remote(meta.at[slot, core], meta.at[slot, core], sm_s.at[slot], sm_r.at[slot], sibling)

    def cot_sib(core):
        return remote(rawa.at[core], rawa.at[core], sa_s.at[0], sa_r.at[0], sibling)

    loads[2].wait()
    cot_sib(c).start()
    loads[0].wait()
    loads[1].wait()
    raw_sib(0, c).start()
    for direction in range(2):
        raw_ring(direction, 0).start()

    expert = lax.broadcasted_iota(jnp.int32, (16, TOK), 0)
    first = jnp.broadcast_to(ids_ref[0:1], (16, TOK)) == expert
    second = jnp.broadcast_to(ids_ref[1:2], (16, TOK)) == expert
    gates = gate_ref[...].astype(F32) * (1.0 / 16.0)
    named = jnp.where(first | second, 1.0, 0.0)
    gate_of = jnp.where(first, jnp.broadcast_to(gates[0:1], (16, TOK)), 0.0) + jnp.where(
        second, jnp.broadcast_to(gates[1:2], (16, TOK)), 0.0)
    token = lax.broadcasted_iota(jnp.int32, (TOK, SPAN), 0)
    place = lax.broadcasted_iota(jnp.int32, (TOK, SPAN), 1)
    taken = (token - place == QT * (y - c)) & (place >= QT * c) & (place < QT * c + QT)
    pick = jnp.where(taken, 1.0, 0.0).astype(BF16)
    named_q = dot_nn(named.astype(BF16), pick)
    gate_q = dot_nn(gate_of.astype(BF16), pick)
    earlier = jnp.where(
        lax.broadcasted_iota(jnp.int32, (SPAN, SPAN), 0) < lax.broadcasted_iota(jnp.int32, (SPAN, SPAN), 1), 1.0, 0.0
    ).astype(BF16)
    rank = dot_nn(named_q.astype(BF16), earlier)
    base = jnp.where(c == 0, 1.0, 1.0 + SL // NC)
    meta[0, c, 0:16] = jnp.where(named_q > 0.5, rank + base, 0.0).astype(BF16)
    meta[0, c, 16:32] = gate_q.astype(BF16)
    meta_sib(0, c).start()
    for direction in range(2):
        meta_ring(direction, 0).start()

    def w2_send(j):
        return remote(w2b.at[0], w2b.at[NY - j], wy_s.at[j - 1, 1], wy_r.at[NY - j - 1, 1], (ep, yrank(j)))

    def w1_send(j):
        return remote(w1b.at[0], w1b.at[NY - j], wy_s.at[j - 1, 0], wy_r.at[NY - j - 1, 0], (ep, yrank(j)))

    def w2_recv(j):
        return remote(w2b.at[0], w2b.at[j], wy_s.at[j - 1, 1], wy_r.at[j - 1, 1], (ep, yrank(j)))

    def w1_recv(j):
        return remote(w1b.at[0], w1b.at[j], wy_s.at[j - 1, 0], wy_r.at[j - 1, 0], (ep, yrank(j)))

    loads[3].wait()
    for j in (2, 1, 3):
        w2_send(j).start()

    def build(slot):
        both = meta[slot, 0].astype(F32) + meta[slot, 1].astype(F32)
        want = lax.broadcasted_iota(jnp.int32, (SL, SPAN), 0).astype(F32) + 1.0
        for k in range(NX):
            row = jnp.where(c == 0, both[2 * k:2 * k + 1], both[2 * k + 1:2 * k + 2])
            gate = jnp.where(c == 0, both[16 + 2 * k:17 + 2 * k], both[17 + 2 * k:18 + 2 * k])
            hit = jnp.broadcast_to(row, (SL, SPAN)) == want
            p_ref[slot, k * SL:(k + 1) * SL] = jnp.where(hit, 1.0, 0.0).astype(BF16)
            pg_ref[slot, k * SL:(k + 1) * SL] = jnp.where(
                hit, jnp.broadcast_to(gate, (SL, SPAN)), 0.0).astype(BF16)

    def xrows(k):
        return pl.ds(pl.multiple_of(k * SL, 16), SL)

    def packb_send(slot, k):
        return remote(packb.at[slot, xrows(xrank(k))], rowsb.at[slot, xrows(x)], xb_s.at[slot, k - 1],
                      xb_r.at[slot, k - 1], xdev(k))

    def packb_recv(slot, k):
        return remote(packb.at[slot, xrows(xrank(k))], rowsb.at[slot, xrows(xrank(NX - k))], xb_s.at[slot, k - 1],
                      xb_r.at[slot, k - 1], xdev(k))

    def packa_send(k):
        return remote(packa.at[xrows(xrank(k))], rowsa.at[0, xrows(x)], xa_s.at[k - 1], xa_r.at[k - 1], xdev(k))

    def packa_recv(k):
        return remote(packa.at[xrows(xrank(k))], rowsa.at[0, xrows(xrank(NX - k))], xa_s.at[k - 1], xa_r.at[k - 1],
                      xdev(k))

    def pack_b(slot):
        packb[slot, :, 0:DIN] = dot_nn(p_ref[slot], rawb[slot, :, :, 0:DIN].reshape(SPAN, DIN)).astype(BF16)
        packb[slot, :, DIN:WB] = dot_nn(pg_ref[slot], rawb[slot, :, :, DIN:WB].reshape(SPAN, CB)).astype(BF16)

    def send_b(slot):
        for k in (2, 1, 3):
            packb_send(slot, k).start()
        rowsb[slot, xrows(x)] = packb[slot, xrows(x)]

    meta_sib(0, 1 - c).wait_recv()
    build(0)
    cot_sib(1 - c).wait_recv()
    packa[...] = dot_nn(pg_ref[0], rawa[...].reshape(SPAN, WA)).astype(BF16)
    for k in (2, 1, 3):
        packa_send(k).start()
    rowsa[0, xrows(x)] = packa[xrows(x)]

    def raw_pass(step):
        for direction in range(2):
            raw_ring(direction, step - 1).wait_recv()
            if step <= 3:
                raw_ring(direction, step).start()
            if has_meta(direction, step - 1):
                meta_ring(direction, step - 1).wait_recv()
                if step <= 3 and has_meta(direction, step):
                    meta_ring(direction, step).start()
            if step <= 3:
                slot = slots(direction, step - 1)[1]
                raw_sib(slot, c).start()
                meta_sib(slot, c).start()
        if step == 4:
            raw_sib(7, c).start()
            meta_sib(7, c).start()

    def sib_pass(slot):
        raw_sib(slot, 1 - c).wait_recv()
        meta_sib(slot, 1 - c).wait_recv()
        build(slot)
        pack_b(slot)

    def row_start(step, h):
        for direction in range(2):
            if h in row_halves(direction, step):
                row_ring(direction, step, h).start()

    def row_pass(step, h):
        for direction in range(2):
            if h in row_halves(direction, step - 1):
                row_ring(direction, step - 1, h).wait_recv()
                if step <= 3 and h in row_halves(direction, step):
                    row_ring(direction, step, h).start()

    raw_sib(0, 1 - c).wait_recv()
    pack_b(0)
    raw_pass(1)
    loads[4].wait()
    w1b[0] = w1v[...].astype(F32).T.astype(BF16)
    for j in (2, 1, 3):
        w1_send(j).start()
    sib_pass(1)
    sib_pass(2)
    raw_pass(2)
    for k in (1, 3, 2):
        packa_recv(k).wait_recv()
    row_start(0, 0)
    send_b(0)
    send_b(1)
    send_b(2)
    sib_pass(3)
    sib_pass(4)
    raw_pass(3)
    row_start(0, 1)
    send_b(3)
    send_b(4)
    sib_pass(5)
    sib_pass(6)
    send_b(5)
    send_b(6)
    row_pass(1, 0)
    raw_pass(4)
    sib_pass(7)
    send_b(7)
    row_pass(1, 1)

    def forward(s0, n):
        for slot in range(s0, s0 + n):
            for k in (1, 3, 2):
                packb_recv(slot, k).wait_recv()
        rows = slice(s0 * G, (s0 + n) * G)

        @pl.loop(0, 2)
        def _(h):
            w1 = w1b[pl.ds(2 * h, 2)].reshape(HALF, DIN)
            w2 = w2b[pl.ds(2 * h, 2)].reshape(HALF, DOUT)
            pre = dot_nt(rowsb[s0:s0 + n, :, 0:DIN].reshape(n * G, DIN), w1)
            back = dot_nt(rowsb[s0:s0 + n, :, DIN:WB].reshape(n * G, CB), w2[:, 0:CB])
            back += dot_nt(rowsa[s0:s0 + n].reshape(n * G, WA), w2[:, CB:DOUT])
            act, slope = gelu_parts(pre)
            actb[h, rows] = act.astype(BF16)
            bpb[h, rows] = (back * slope).astype(BF16)

        for half in range(2):
            cols = slice(half * 512, (half + 1) * 512)
            part = dot_nn(bpb[0, rows], w1b[0:2, :, cols].reshape(HALF, 512))
            part += dot_nn(bpb[1, rows], w1b[2:4, :, cols].reshape(HALF, 512))
            pown[s0:s0 + n, half] = part.reshape(n, G, 512)

    for j in (1, 3, 2):
        w2_recv(j).wait_recv()
        w1_recv(j).wait_recv()
    forward(0, 1)
    row_pass(2, 0)
    forward(1, 2)
    row_pass(2, 1)
    row_pass(3, 0)
    forward(3, 2)
    row_pass(3, 1)
    forward(5, 2)
    row_pass(4, 0)
    row_pass(4, 1)
    forward(7, 1)

    def rs(direction, step, ch):
        src, dst = sbuf.at[direction, step, ch], rbuf.at[direction, step, ch]
        if step == 0:
            half = pl.ds(direction * (G // 2), G // 2)
            src, dst = src.at[half], dst.at[half]
        return remote(src, dst, rs_s.at[direction, step, ch], rs_r.at[direction, step, ch],
                      right if direction == 0 else left)

    for ch in range(2):
        for direction in range(2):
            half = slice(direction * (G // 2), (direction + 1) * (G // 2))
            sbuf[direction, 0, ch, half] = pown[7, ch, half].astype(BF16)
            rs(direction, 0, ch).start()

    def rs_pass(step):
        for ch in range(2):
            for direction in range(2):
                slot = 7 - 2 * step + direction
                rs(direction, step - 1, ch).wait_recv()
                if step == 1:
                    got = slice(direction * (G // 2), (direction + 1) * (G // 2))
                    rest = slice((1 - direction) * (G // 2), (2 - direction) * (G // 2))
                    sbuf[direction, step, ch, rest] = pown[slot, ch, rest].astype(BF16)
                else:
                    got = slice(0, G)
                sbuf[direction, step, ch, got] = (
                    pown[slot, ch, got] + rbuf[direction, step - 1, ch, got].astype(F32)
                ).astype(BF16)
                rs(direction, step, ch).start()

    def grad_send(j, ch):
        return remote(gsend.at[j - 1, ch], grecv.at[NY - j - 1, ch], gy_s.at[j - 1, ch], gy_r.at[NY - j - 1, ch],
                      (ep, yrank(j)))

    def grad_recv(j, ch):
        return remote(gsend.at[j - 1, ch], grecv.at[j - 1, ch], gy_s.at[j - 1, ch], gy_r.at[j - 1, ch],
                      (ep, yrank(j)))

    def weight_grads(h, ch):
        left_side = bpb[h] if ch == 0 else actb[h]
        for part in range(2):
            col = part * 512
            if ch == 0:
                right_side = rowsb[:, :, col:col + 512]
            elif ch == 1 and part == 0:
                right_side = rowsb[:, :, DIN:WB]
            else:
                at = (ch - 1) * 1024 + col - CB
                right_side = rowsa[:, :, at:at + 512]
            total = dot_tn(left_side, right_side.reshape(ROWS, 512))
            for i in range(2):
                j = 2 * h + i
                block = total[i * SPAN:(i + 1) * SPAN]
                if j == 0:
                    gown[ch, :, col:col + 512] = block
                else:
                    gsend[j - 1, ch, :, col:col + 512] = block.astype(BF16)
        for i in range(2):
            if 2 * h + i:
                grad_send(2 * h + i, ch).start()

    order = (1, 2, 0)
    weight_grads(1, 1)
    weight_grads(1, 2)
    rs_pass(1)
    weight_grads(1, 0)
    weight_grads(0, 1)
    rs_pass(2)
    weight_grads(0, 2)
    weight_grads(0, 0)
    rs_pass(3)

    def ret_send(k):
        return remote(retb.at[xrows(xrank(k))], retr.at[xrows(x)], rt_s.at[k - 1], rt_r.at[k - 1], xdev(k))

    def ret_recv(k):
        return remote(retb.at[xrows(xrank(k))], retr.at[xrows(xrank(NX - k))], rt_s.at[k - 1], rt_r.at[k - 1], xdev(k))

    for ch in range(2):
        for direction in range(2):
            rs(direction, 3, ch).wait_recv()
        retb[:, ch * 512:(ch + 1) * 512] = (
            pown[0, ch] + rbuf[0, 3, ch].astype(F32) + rbuf[1, 3, ch].astype(F32)
        ).astype(BF16)
    for k in (2, 1, 3):
        ret_send(k).start()
    retr[xrows(x)] = retb[xrows(x)]
    for k in (1, 3, 2):
        ret_recv(k).wait_recv()
    sibs[...] = dot_tn(p_ref[0], retr[...]).reshape(NC, QT, DIN)
    other = remote(sibs.at[1 - c], sibr, s2_s.at[0], s2_r.at[0], sibling)
    other.start()
    other.wait_recv()
    total = (sibs[c] + sibr[...]).astype(BF16)
    for q in range(NY):
        giny[q] = total[:, q * QX:(q + 1) * QX]

    def out_send(j):
        return remote(giny.at[yrank(j)], gout.at[quarter], yo_s.at[j - 1], yo_r.at[j - 1], (ep, yrank(j)))

    def out_recv(j):
        return remote(giny.at[yrank(j)], gout.at[pl.ds(pl.multiple_of(yrank(NY - j) * QT, QT), QT)], yo_s.at[j - 1], yo_r.at[j - 1], (ep, yrank(j)))

    for j in (2, 1, 3):
        out_send(j).start()
    gout[quarter] = giny[y]

    stores = [
        pltpu.make_async_copy(gv1, g1_ref.at[0], st.at[0]),
        pltpu.make_async_copy(gv2.at[:, pl.ds(0, 1024)], g2_ref.at[0, :, pl.ds(0, 1024)], st.at[1]),
        pltpu.make_async_copy(gv2.at[:, pl.ds(1024, 1024)], g2_ref.at[0, :, pl.ds(1024, 1024)], st.at[2]),
        pltpu.make_async_copy(gout, gin_ref, st.at[3]),
    ]
    for ch in order:
        for j in (1, 3, 2):
            grad_recv(j, ch).wait_recv()
        total = (
            gown[ch] + grecv[0, ch].astype(F32) + grecv[1, ch].astype(F32) + grecv[2, ch].astype(F32)
        ) * grad_scale
        if ch == 0:
            gv1[...] = total.T.astype(BF16)
            stores[0].start()
        else:
            gv2[:, (ch - 1) * 1024:ch * 1024] = total.astype(BF16)
            stores[ch].start()

    for j in (1, 3, 2):
        out_recv(j).wait_recv()
    stores[3].start()
    for store in stores:
        store.wait()

    for direction in range(2):
        for step in range(4):
            raw_ring(direction, step).wait_send()
            if has_meta(direction, step):
                meta_ring(direction, step).wait_send()
            for h in row_halves(direction, step):
                row_ring(direction, step, h).wait_send()
            for ch in range(2):
                rs(direction, step, ch).wait_send()
    for slot in range(8):
        raw_sib(slot, c).wait_send()
        meta_sib(slot, c).wait_send()
        for k in range(1, NX):
            packb_send(slot, k).wait_send()
    cot_sib(c).wait_send()
    other.wait_send()
    for k in range(1, NX):
        packa_send(k).wait_send()
        ret_send(k).wait_send()
    for j in range(1, NY):
        w1_send(j).wait_send()
        w2_send(j).wait_send()
        out_send(j).wait_send()
        for ch in range(3):
            grad_send(j, ch).wait_send()


def hand_over(a_ref, b_ref, c_ref, a_out, b_out, c_out, a_mid, b_mid, c_mid, sems):
    trios = ((a_ref, a_mid, a_out), (b_ref, b_mid, b_out), (c_ref, c_mid, c_out))
    loads = [pltpu.make_async_copy(src, mid, sems.at[0, i]) for i, (src, mid, _) in enumerate(trios)]
    stores = [pltpu.make_async_copy(mid, dst, sems.at[1, i]) for i, (_, mid, dst) in enumerate(trios)]
    for load in loads:
        load.start()
    for load, store in zip(loads, stores):
        load.wait()
        store.start()
    for store in stores:
        store.wait()


def shards(features, cotangent, expert_ids, gate_levels, w_in, w_out):
    tokens = features.shape[0] * lax.axis_size("ep")
    grad_scale = 1.0 / math.sqrt(2.0 * tokens / E)
    vm = pl.BlockSpec(memory_space=pltpu.VMEM)
    hbm = pl.BlockSpec(memory_space=pl.ANY)
    dma = pltpu.SemaphoreType.DMA

    def pair(*shape):
        return [dma(shape), dma(shape)]

    grads = pl.pallas_call(
        functools.partial(kernel, grad_scale),
        out_shape=(
            jax.ShapeDtypeStruct((TOK, QX), BF16),
            jax.ShapeDtypeStruct((1, DIN, SPAN), BF16),
            jax.ShapeDtypeStruct((1, SPAN, DOUT), BF16),
        ),
        in_specs=[hbm, hbm, vm, vm, hbm, hbm],
        out_specs=(hbm, hbm, hbm),
        scratch_shapes=[
            pltpu.VMEM((NZ, NC, QT, WB), BF16),
            pltpu.VMEM((NC, QT, WA), BF16),
            pltpu.VMEM((NZ, NC, 32, SPAN), BF16),
            pltpu.VMEM((NZ, G, SPAN), BF16),
            pltpu.VMEM((NZ, G, SPAN), BF16),
            pltpu.VMEM((G, WA), BF16),
            pltpu.VMEM((NZ, G, WB), BF16),
            pltpu.VMEM((NZ, G, WA), BF16),
            pltpu.VMEM((NZ, G, WB), BF16),
            pltpu.VMEM((DIN, SPAN), BF16),
            pltpu.VMEM((NY, SPAN, DIN), BF16),
            pltpu.VMEM((NY, SPAN, DOUT), BF16),
            pltpu.VMEM((2, ROWS, HALF), BF16),
            pltpu.VMEM((2, ROWS, HALF), BF16),
            pltpu.VMEM((NZ, 2, G, 512), F32),
            pltpu.VMEM((2, 4, 2, G, 512), BF16),
            pltpu.VMEM((2, 4, 2, G, 512), BF16),
            pltpu.VMEM((3, SPAN, 1024), F32),
            pltpu.VMEM((NY - 1, 3, SPAN, 1024), BF16),
            pltpu.VMEM((NY - 1, 3, SPAN, 1024), BF16),
            pltpu.VMEM((G, DIN), BF16),
            pltpu.VMEM((G, DIN), BF16),
            pltpu.VMEM((NC, QT, DIN), F32),
            pltpu.VMEM((QT, DIN), F32),
            pltpu.VMEM((NY, QT, QX), BF16),
            pltpu.VMEM((TOK, QX), BF16),
            pltpu.VMEM((DIN, SPAN), BF16),
            pltpu.VMEM((SPAN, DOUT), BF16),
            dma((5,)),
            dma((4,)),
            *pair(2, 4), *pair(2, 4), *pair(8), *pair(8), *pair(1),
            *pair(8, 3), *pair(3), *pair(2, 4, 2), *pair(3, 2), *pair(2, 4, 2), *pair(3, 3),
            *pair(3), *pair(1), *pair(3),
        ],
        compiler_params=pltpu.CompilerParams(
            collective_id=0, has_side_effects=True, vmem_limit_bytes=60 * 1024 * 1024
        ),
        cost_estimate=pl.CostEstimate(flops=11_300_000_000, bytes_accessed=5_000_000, transcendentals=0),
        name="moe_backward",
    )(features, cotangent, expert_ids.T, gate_levels.T, w_in, w_out)
    return pl.pallas_call(
        hand_over,
        out_shape=tuple(jax.ShapeDtypeStruct(g.shape, g.dtype) for g in grads),
        in_specs=[hbm] * 3,
        out_specs=(hbm,) * 3,
        scratch_shapes=[*(pltpu.VMEM(g.shape, g.dtype) for g in grads), dma((2, 3))],
        name="hand_over",
    )(*grads)


def solution(mesh):
    return jax.shard_map(
        shards,
        mesh=mesh,
        in_specs=(
            P("ep", None),
            P("ep", None),
            P("ep", None),
            P("ep", None),
            P("ep", None, "tp"),
            P("ep", "tp", None),
        ),
        out_specs=(P("ep", "tp"), P("ep", None, "tp"), P("ep", "tp", None)),
        check_vma=False,
    )
```

```python
import functools
import math

import jax
import jax.numpy as jnp
from jax import lax
from jax.experimental import pallas as pl
from jax.experimental.pallas import tpu as pltpu
from jax.sharding import PartitionSpec as P

MESH = pl.DeviceIdType.MESH
E = 8
NZ, NX, NC, NY = 8, 4, 2, 4
TOK = 256
QT = TOK // NY
DIN = 1024
DOUT = 2048
SPAN = 128
QX = DIN // NY
SL = 48
G = NX * SL
CB = 512
WB = DIN + CB
WA = DOUT - CB
HALF = 2 * SPAN
ROWS = NZ * G
F32 = jnp.float32
BF16 = jnp.bfloat16


def dot_nn(a, b):
    return lax.dot_general(a, b, (((1,), (0,)), ((), ())), preferred_element_type=F32)


def dot_nt(a, b):
    return lax.dot_general(a, b, (((1,), (1,)), ((), ())), preferred_element_type=F32)


def dot_tn(a, b):
    return lax.dot_general(a, b, (((0,), (0,)), ((), ())), preferred_element_type=F32)


def gelu_parts(v):
    k = math.sqrt(2.0 / math.pi)
    vv = v * v
    t = jnp.tanh(k * (v + 0.044715 * (v * vv)))
    half = 0.5 * (1.0 + t)
    act = v * half
    slope = half + 0.5 * v * (1.0 - t * t) * (k * (1.0 + 3.0 * 0.044715 * vv))
    return act, slope


def kernel(
    grad_scale,
    x_ref, dy_ref, ids_hbm, gate_hbm, w1_ref, w2_ref,
    gin_ref, g1_ref, g2_ref,
    rawb, rawa, meta, p_ref, pg_ref, p_all, packa, packb, rowsa, rowsb,
    ids_ref, gate_ref, w1v, w1b, w2b, actb, bpb, pown, sbuf, rbuf, gown, gfar, gnear, ghalf, gsend, grecv,
    retb, retr, tokens, giny, gout, gv1, gv2,
    ld, st, zb_s, zb_r, zm_s, zm_r, sb_s, sb_r, sm_s, sm_r, sa_s, sa_r,
    xb_s, xb_r, xa_s, xa_r, za_s, za_r, wy_s, wy_r, rs_s, rs_r, gh_s, gh_r, gy_s, gy_r,
    rt_s, rt_r, yo_s, yo_r,
):
    ep = lax.axis_index("ep")
    y = lax.axis_index("tp")
    z = ep // E
    me = lax.rem(ep, E)
    x = me // NC
    c = lax.rem(me, NC)
    right = (lax.rem(z + 1, NZ) * E + me, y)
    left = (lax.rem(z + NZ - 1, NZ) * E + me, y)
    sibling = (z * E + me + 1 - 2 * c, y)

    def xrank(k):
        return lax.rem(x + k, NX)

    def xdev(k):
        return (z * E + xrank(k) * NC + c, y)

    def yrank(k):
        return lax.rem(y + k, NY)

    def plane(m):
        return (z * E + lax.rem(me + m, E), y)

    def remote(src, dst, ss, rs, dev):
        return pltpu.make_async_remote_copy(
            src_ref=src, dst_ref=dst, send_sem=ss, recv_sem=rs, device_id=dev, device_id_type=MESH
        )

    quarter = pl.ds(pl.multiple_of(y * QT, QT), QT)
    loads = [
        pltpu.make_async_copy(x_ref.at[quarter], rawb.at[0, c, :, pl.ds(0, DIN)], ld.at[0]),
        pltpu.make_async_copy(dy_ref.at[quarter, pl.ds(0, CB)], rawb.at[0, c, :, pl.ds(DIN, CB)], ld.at[1]),
        pltpu.make_async_copy(dy_ref.at[quarter, pl.ds(CB, WA)], rawa.at[c], ld.at[2]),
        pltpu.make_async_copy(w2_ref.at[0], w2b.at[0], ld.at[3]),
        pltpu.make_async_copy(w1_ref.at[0], w1v, ld.at[4]),
        pltpu.make_async_copy(ids_hbm, ids_ref, ld.at[5]),
        pltpu.make_async_copy(gate_hbm, gate_ref, ld.at[6]),
    ]
    for load in loads:
        load.start()

    bar = pltpu.get_barrier_semaphore()
    partners = [left, right]
    partners += [plane(m) for m in range(1, E)] + [(ep, yrank(k)) for k in range(1, NY)]
    for dev in partners:
        pl.semaphore_signal(bar, inc=1, device_id=dev, device_id_type=MESH)
    pl.semaphore_wait(bar, len(partners))

    def slots(direction, step):
        src = 0 if step == 0 else 2 * step - 1 + direction
        return src, (7 if step == 3 else 2 * step + 1 + direction)

    def toward(direction):
        return left if direction == 0 else right

    def raw_ring(direction, step):
        s, d = slots(direction, step)
        src, dst = rawb.at[s, c], rawb.at[d, c]
        if step == 3:
            half = pl.ds(direction * (QT // 2), QT // 2)
            src, dst = src.at[half], dst.at[half]
        return remote(src, dst, zb_s.at[direction, step], zb_r.at[direction, step], toward(direction))

    def meta_ring(direction, step):
        s, d = slots(direction, step)
        return remote(meta.at[s, c], meta.at[d, c], zm_s.at[direction, step], zm_r.at[direction, step],
                      toward(direction))

    def has_meta(direction, step):
        return step < 3 or direction == 0

    def row_ring(direction, step, k):
        s, d = slots(direction, step)
        piece = pl.ds(pl.multiple_of(xrank(k) * SL, 16), SL)
        return remote(rowsa.at[s, piece], rowsa.at[d, piece], za_s.at[direction, step, k], za_r.at[direction, step, k],
                      toward(direction))

    def row_pieces(direction, step):
        if step == 3:
            return (0, 2) if direction == 0 else (1, 3)
        return (0, 1, 3, 2)

    def raw_sib(slot, core):
        return remote(rawb.at[slot, core], rawb.at[slot, core], sb_s.at[slot], sb_r.at[slot], sibling)

    def meta_sib(slot, core):
        return remote(meta.at[slot, core], meta.at[slot, core], sm_s.at[slot], sm_r.at[slot], sibling)

    def cot_sib(core):
        return remote(rawa.at[core], rawa.at[core], sa_s.at[0], sa_r.at[0], sibling)

    loads[2].wait()
    cot_sib(c).start()
    loads[0].wait()
    loads[1].wait()
    raw_sib(0, c).start()
    for direction in range(2):
        raw_ring(direction, 0).start()

    loads[5].wait()
    loads[6].wait()
    expert = lax.broadcasted_iota(jnp.int32, (16, TOK), 0)
    first = jnp.broadcast_to(ids_ref[0:1], (16, TOK)) == expert
    second = jnp.broadcast_to(ids_ref[1:2], (16, TOK)) == expert
    gates = gate_ref[...].astype(F32) * (1.0 / 16.0)
    named = jnp.where(first | second, 1.0, 0.0)
    gate_of = jnp.where(first, jnp.broadcast_to(gates[0:1], (16, TOK)), 0.0) + jnp.where(
        second, jnp.broadcast_to(gates[1:2], (16, TOK)), 0.0)
    token = lax.broadcasted_iota(jnp.int32, (TOK, SPAN), 0)
    place = lax.broadcasted_iota(jnp.int32, (TOK, SPAN), 1)
    taken = (token - place == QT * (y - c)) & (place >= QT * c) & (place < QT * c + QT)
    pick = jnp.where(taken, 1.0, 0.0).astype(BF16)
    named_q = dot_nn(named.astype(BF16), pick)
    gate_q = dot_nn(gate_of.astype(BF16), pick)
    earlier = jnp.where(
        lax.broadcasted_iota(jnp.int32, (SPAN, SPAN), 0) < lax.broadcasted_iota(jnp.int32, (SPAN, SPAN), 1), 1.0, 0.0
    ).astype(BF16)
    rank = dot_nn(named_q.astype(BF16), earlier)
    base = jnp.where(c == 0, 1.0, 1.0 + SL // NC)
    meta[0, c, 0:16] = jnp.where(named_q > 0.5, rank + base, 0.0).astype(BF16)
    meta[0, c, 16:32] = gate_q.astype(BF16)
    meta_sib(0, c).start()
    for direction in range(2):
        meta_ring(direction, 0).start()

    def w2_send(j):
        return remote(w2b.at[0], w2b.at[NY - j], wy_s.at[j - 1, 1], wy_r.at[NY - j - 1, 1], (ep, yrank(j)))

    def w1_send(j):
        return remote(w1b.at[0], w1b.at[NY - j], wy_s.at[j - 1, 0], wy_r.at[NY - j - 1, 0], (ep, yrank(j)))

    def w2_recv(j):
        return remote(w2b.at[0], w2b.at[j], wy_s.at[j - 1, 1], wy_r.at[j - 1, 1], (ep, yrank(j)))

    def w1_recv(j):
        return remote(w1b.at[0], w1b.at[j], wy_s.at[j - 1, 0], wy_r.at[j - 1, 0], (ep, yrank(j)))

    loads[3].wait()
    for j in (2, 1, 3):
        w2_send(j).start()

    def build(slot):
        both = meta[slot, 0].astype(F32) + meta[slot, 1].astype(F32)
        want = lax.broadcasted_iota(jnp.int32, (SL, SPAN), 0).astype(F32) + 1.0
        for k in range(NX):
            row = jnp.where(c == 0, both[2 * k:2 * k + 1], both[2 * k + 1:2 * k + 2])
            gate = jnp.where(c == 0, both[16 + 2 * k:17 + 2 * k], both[17 + 2 * k:18 + 2 * k])
            hit = jnp.broadcast_to(row, (SL, SPAN)) == want
            chosen = jnp.where(hit, 1.0, 0.0).astype(BF16)
            p_ref[slot, k * SL:(k + 1) * SL] = chosen
            if slot == 0:
                p_all[0, k * SL:(k + 1) * SL] = chosen
                row = jnp.where(c == 0, both[2 * k + 1:2 * k + 2], both[2 * k:2 * k + 1])
                chosen = jnp.where(jnp.broadcast_to(row, (SL, SPAN)) == want, 1.0, 0.0).astype(BF16)
                p_all[1, k * SL:(k + 1) * SL] = chosen
            pg_ref[slot, k * SL:(k + 1) * SL] = jnp.where(
                hit, jnp.broadcast_to(gate, (SL, SPAN)), 0.0).astype(BF16)

    def xrows(k):
        return pl.ds(pl.multiple_of(k * SL, 16), SL)

    def packb_send(slot, k):
        return remote(packb.at[slot, xrows(xrank(k))], rowsb.at[slot, xrows(x)], xb_s.at[slot, k - 1],
                      xb_r.at[slot, k - 1], xdev(k))

    def packb_recv(slot, k):
        return remote(packb.at[slot, xrows(xrank(k))], rowsb.at[slot, xrows(xrank(NX - k))], xb_s.at[slot, k - 1],
                      xb_r.at[slot, k - 1], xdev(k))

    def packa_send(k):
        return remote(packa.at[xrows(xrank(k))], rowsa.at[0, xrows(x)], xa_s.at[k - 1], xa_r.at[k - 1], xdev(k))

    def packa_recv(k):
        return remote(packa.at[xrows(xrank(k))], rowsa.at[0, xrows(xrank(NX - k))], xa_s.at[k - 1], xa_r.at[k - 1],
                      xdev(k))

    def pack_b(slot):
        packb[slot, :, 0:DIN] = dot_nn(p_ref[slot], rawb[slot, :, :, 0:DIN].reshape(SPAN, DIN)).astype(BF16)
        packb[slot, :, DIN:WB] = dot_nn(pg_ref[slot], rawb[slot, :, :, DIN:WB].reshape(SPAN, CB)).astype(BF16)

    def send_b(slot):
        for k in (2, 1, 3):
            packb_send(slot, k).start()
        rowsb[slot, xrows(x)] = packb[slot, xrows(x)]

    meta_sib(0, 1 - c).wait_recv()
    build(0)
    cot_sib(1 - c).wait_recv()
    packa[...] = dot_nn(pg_ref[0], rawa[...].reshape(SPAN, WA)).astype(BF16)
    for k in (1, 3, 2):
        packa_send(k).start()
    rowsa[0, xrows(x)] = packa[xrows(x)]

    def raw_pass(step):
        for direction in range(2):
            raw_ring(direction, step - 1).wait_recv()
            if step <= 3:
                raw_ring(direction, step).start()
            if has_meta(direction, step - 1):
                meta_ring(direction, step - 1).wait_recv()
                if step <= 3 and has_meta(direction, step):
                    meta_ring(direction, step).start()
            if step <= 3:
                slot = slots(direction, step - 1)[1]
                raw_sib(slot, c).start()
                meta_sib(slot, c).start()
        if step == 4:
            raw_sib(7, c).start()
            meta_sib(7, c).start()

    def sib_pass(slot):
        raw_sib(slot, 1 - c).wait_recv()
        meta_sib(slot, 1 - c).wait_recv()
        build(slot)
        pack_b(slot)

    def row_start(k):
        for direction in range(2):
            row_ring(direction, 0, k).start()

    def row_pass(step, k):
        for direction in range(2):
            if k in row_pieces(direction, step - 1):
                row_ring(direction, step - 1, k).wait_recv()
                if step <= 3 and k in row_pieces(direction, step):
                    row_ring(direction, step, k).start()

    row_start(0)
    raw_pass(1)
    raw_sib(0, 1 - c).wait_recv()
    pack_b(0)
    packa_recv(3).wait_recv()
    row_start(1)
    packa_recv(1).wait_recv()
    row_start(3)
    send_b(0)
    sib_pass(1)
    sib_pass(2)
    send_b(1)
    send_b(2)
    packa_recv(2).wait_recv()
    row_start(2)
    raw_pass(2)
    loads[4].wait()
    w1b[0] = w1v[...].astype(F32).T.astype(BF16)
    for j in (2, 1, 3):
        w1_send(j).start()
    sib_pass(3)
    sib_pass(4)
    send_b(3)
    send_b(4)
    row_pass(1, 0)
    raw_pass(3)
    row_pass(1, 1)
    sib_pass(5)
    sib_pass(6)
    send_b(5)
    send_b(6)
    row_pass(1, 3)
    raw_pass(4)
    row_pass(1, 2)
    sib_pass(7)
    send_b(7)
    row_pass(2, 0)
    row_pass(2, 1)

    def forward(s0, n):
        for slot in range(s0, s0 + n):
            for k in (1, 3, 2):
                packb_recv(slot, k).wait_recv()
        rows = slice(s0 * G, (s0 + n) * G)

        @pl.loop(0, 2)
        def _(h):
            w1 = w1b[pl.ds(2 * h, 2)].reshape(HALF, DIN)
            w2 = w2b[pl.ds(2 * h, 2)].reshape(HALF, DOUT)
            pre = dot_nt(rowsb[s0:s0 + n, :, 0:DIN].reshape(n * G, DIN), w1)
            back = dot_nt(rowsb[s0:s0 + n, :, DIN:WB].reshape(n * G, CB), w2[:, 0:CB])
            back += dot_nt(rowsa[s0:s0 + n].reshape(n * G, WA), w2[:, CB:DOUT])
            act, slope = gelu_parts(pre)
            actb[h, rows] = act.astype(BF16)
            bpb[h, rows] = (back * slope).astype(BF16)

        for q in range(NY):
            cols = slice(q * QX, (q + 1) * QX)
            part = dot_nn(bpb[0, rows], w1b[0:2, :, cols].reshape(HALF, QX))
            part += dot_nn(bpb[1, rows], w1b[2:4, :, cols].reshape(HALF, QX))
            pown[s0:s0 + n, q] = part.reshape(n, G, QX)

    for j in (1, 3, 2):
        w2_recv(j).wait_recv()
        w1_recv(j).wait_recv()
    forward(0, 1)
    row_pass(2, 3)
    row_pass(2, 2)
    row_pass(3, 0)
    forward(1, 2)
    row_pass(3, 1)
    row_pass(3, 3)
    row_pass(3, 2)
    forward(3, 2)
    forward(5, 2)
    for k in range(NX):
        row_pass(4, k)
    forward(7, 1)

    def rs(direction, step, ch):
        src, dst = sbuf.at[direction, step, ch], rbuf.at[direction, step, ch]
        if step == 0:
            half = pl.ds(direction * (G // 2), G // 2)
            src, dst = src.at[half], dst.at[half]
        return remote(src, dst, rs_s.at[direction, step, ch], rs_r.at[direction, step, ch],
                      right if direction == 0 else left)

    turns = [yrank(j) for j in (2, 1, 3, 0)]
    for ch in turns:
        for direction in range(2):
            half = slice(direction * (G // 2), (direction + 1) * (G // 2))
            sbuf[direction, 0, ch, half] = pown[7, ch, half].astype(BF16)
            rs(direction, 0, ch).start()

    def rs_pass(step, ch):
        for direction in range(2):
            slot = 7 - 2 * step + direction
            rs(direction, step - 1, ch).wait_recv()
            if step == 1:
                got = slice(direction * (G // 2), (direction + 1) * (G // 2))
                rest = slice((1 - direction) * (G // 2), (2 - direction) * (G // 2))
                sbuf[direction, step, ch, rest] = pown[slot, ch, rest].astype(BF16)
            else:
                got = slice(0, G)
            sbuf[direction, step, ch, got] = (
                pown[slot, ch, got] + rbuf[direction, step - 1, ch, got].astype(F32)
            ).astype(BF16)
            rs(direction, step, ch).start()

    ways = (1, NY - 1)

    def half_rows(way):
        return pl.ds(way * (SPAN // 2), SPAN // 2)

    def grad_half(way, ch):
        return remote(gfar.at[ch, half_rows(way)], ghalf.at[ch, half_rows(way)], gh_s.at[way, ch], gh_r.at[way, ch],
                      (ep, yrank(ways[way])))

    def grad_send(way, ch):
        return remote(gsend.at[way, ch], grecv.at[way, ch], gy_s.at[way, ch], gy_r.at[way, ch], (ep, yrank(ways[way])))

    def grad_near(way, ch):
        grad_half(way, ch).wait_recv()
        got = half_rows(way)
        rest = half_rows(1 - way)
        gsend[way, ch, rest] = gnear[way, ch, rest].astype(BF16)
        gsend[way, ch, got] = (gnear[way, ch, got] + ghalf[ch, got].astype(F32)).astype(BF16)
        grad_send(way, ch).start()

    def weight_grads(h, ch):
        left_side = bpb[h] if ch == 0 else actb[h]
        for part in range(2):
            col = part * 512
            if ch == 0:
                right_side = rowsb[:, :, col:col + 512]
            elif ch == 1 and part == 0:
                right_side = rowsb[:, :, DIN:WB]
            else:
                at = (ch - 1) * 1024 + col - CB
                right_side = rowsa[:, :, at:at + 512]
            total = dot_tn(left_side, right_side.reshape(ROWS, 512))
            for i in range(2):
                j = 2 * h + i
                block = total[i * SPAN:(i + 1) * SPAN]
                if j == 0:
                    gown[ch, :, col:col + 512] = block
                elif j == 2:
                    gfar[ch, :, col:col + 512] = block.astype(BF16)
                else:
                    gnear[j // 2, ch, :, col:col + 512] = block
        for way in range(2):
            if h == 1:
                grad_half(way, ch).start()
            else:
                grad_near(way, ch)

    weight_grads(1, 1)
    rs_pass(1, turns[0])
    weight_grads(1, 2)
    rs_pass(1, turns[1])
    rs_pass(1, turns[2])
    weight_grads(1, 0)
    rs_pass(1, turns[3])
    weight_grads(0, 1)
    rs_pass(2, turns[0])
    weight_grads(0, 2)
    rs_pass(2, turns[1])
    weight_grads(0, 0)
    rs_pass(2, turns[2])
    rs_pass(2, turns[3])
    for ch in turns:
        rs_pass(3, ch)

    def ret_send(m, ch):
        to = lax.rem(me + m, E) // NC
        return remote(retb.at[ch, xrows(to)], retr.at[ch, m % 2, xrows(x)], rt_s.at[m - 1, ch], rt_r.at[m - 1, ch],
                      plane(m))

    def ret_recv(m, ch):
        source = lax.rem(me + E - m, E) // NC
        return remote(retb.at[ch, xrows(x)], retr.at[ch, m % 2, xrows(source)], rt_s.at[m - 1, ch], rt_r.at[m - 1, ch],
                      plane(m))

    def out_send(j):
        return remote(giny.at[yrank(j)], gout.at[quarter], yo_s.at[j - 1], yo_r.at[j - 1], (ep, yrank(j)))

    def out_recv(j):
        return remote(giny.at[yrank(j)], gout.at[pl.ds(pl.multiple_of(yrank(NY - j) * QT, QT), QT)], yo_s.at[j - 1],
                      yo_r.at[j - 1], (ep, yrank(j)))

    far_first = (4, 3, 5, 2, 6, 1, 7)

    def tail_rows(j):
        ch = yrank(j)
        for direction in range(2):
            rs(direction, 3, ch).wait_recv()
        retb[ch] = (pown[0, ch] + rbuf[0, 3, ch].astype(F32) + rbuf[1, 3, ch].astype(F32)).astype(BF16)
        for m in far_first:
            ret_send(m, ch).start()
        retr[ch, 0, xrows(x)] = retb[ch, xrows(x)]

    def tail_tokens(j):
        ch = yrank(j)
        for m in far_first:
            ret_recv(m, ch).wait_recv()
        tokens[...] = dot_tn(p_all[...].reshape(2 * G, SPAN), retr[ch].reshape(2 * G, QX)).reshape(NC, QT, QX)
        if j:
            giny[ch] = tokens[c].astype(BF16)
            out_send(j).start()
        else:
            gout[quarter] = tokens[c].astype(BF16)

    stores = [
        pltpu.make_async_copy(gv1, g1_ref.at[0], st.at[0]),
        pltpu.make_async_copy(gv2.at[:, pl.ds(0, 1024)], g2_ref.at[0, :, pl.ds(0, 1024)], st.at[1]),
        pltpu.make_async_copy(gv2.at[:, pl.ds(1024, 1024)], g2_ref.at[0, :, pl.ds(1024, 1024)], st.at[2]),
        pltpu.make_async_copy(gout, gin_ref, st.at[3]),
    ]

    def finish(ch):
        for way in range(2):
            grad_send(way, ch).wait_recv()
        total = (gown[ch] + grecv[0, ch].astype(F32) + grecv[1, ch].astype(F32)) * grad_scale
        if ch == 0:
            gv1[...] = total.T.astype(BF16)
        else:
            gv2[:, (ch - 1) * 1024:ch * 1024] = total.astype(BF16)
        stores[ch].start()

    finish(1)
    tail_rows(2)
    finish(2)
    tail_rows(1)
    tail_tokens(2)
    finish(0)
    tail_rows(3)
    tail_tokens(1)
    tail_rows(0)
    tail_tokens(3)
    tail_tokens(0)
    for j in (1, 3, 2):
        out_recv(j).wait_recv()
    stores[3].start()
    for store in stores:
        store.wait()

    for direction in range(2):
        for step in range(4):
            raw_ring(direction, step).wait_send()
            if has_meta(direction, step):
                meta_ring(direction, step).wait_send()
            for k in row_pieces(direction, step):
                row_ring(direction, step, k).wait_send()
            for ch in range(NY):
                rs(direction, step, ch).wait_send()
    for slot in range(8):
        raw_sib(slot, c).wait_send()
        meta_sib(slot, c).wait_send()
        for k in range(1, NX):
            packb_send(slot, k).wait_send()
    cot_sib(c).wait_send()
    for k in range(1, NX):
        packa_send(k).wait_send()
    for m in range(1, E):
        for ch in range(NY):
            ret_send(m, ch).wait_send()
    for j in range(1, NY):
        w1_send(j).wait_send()
        w2_send(j).wait_send()
        out_send(j).wait_send()
    for way in range(2):
        for ch in range(3):
            grad_half(way, ch).wait_send()
            grad_send(way, ch).wait_send()


def hand_over(a_ref, b_ref, c_ref, a_out, b_out, c_out, a_mid, b_mid, c_mid, sems):
    trios = ((a_ref, a_mid, a_out), (b_ref, b_mid, b_out), (c_ref, c_mid, c_out))
    loads = [pltpu.make_async_copy(src, mid, sems.at[0, i]) for i, (src, mid, _) in enumerate(trios)]
    stores = [pltpu.make_async_copy(mid, dst, sems.at[1, i]) for i, (_, mid, dst) in enumerate(trios)]
    for load in loads:
        load.start()
    for load, store in zip(loads, stores):
        load.wait()
        store.start()
    for store in stores:
        store.wait()


def shards(features, cotangent, expert_ids, gate_levels, w_in, w_out):
    tokens = features.shape[0] * lax.axis_size("ep")
    grad_scale = 1.0 / math.sqrt(2.0 * tokens / E)
    hbm = pl.BlockSpec(memory_space=pl.ANY)
    dma = pltpu.SemaphoreType.DMA

    def pair(*shape):
        return [dma(shape), dma(shape)]

    grads = pl.pallas_call(
        functools.partial(kernel, grad_scale),
        out_shape=(
            jax.ShapeDtypeStruct((TOK, QX), BF16),
            jax.ShapeDtypeStruct((1, DIN, SPAN), BF16),
            jax.ShapeDtypeStruct((1, SPAN, DOUT), BF16),
        ),
        in_specs=[hbm] * 6,
        out_specs=(hbm, hbm, hbm),
        scratch_shapes=[
            pltpu.VMEM((NZ, NC, QT, WB), BF16),
            pltpu.VMEM((NC, QT, WA), BF16),
            pltpu.VMEM((NZ, NC, 32, SPAN), BF16),
            pltpu.VMEM((NZ, G, SPAN), BF16),
            pltpu.VMEM((NZ, G, SPAN), BF16),
            pltpu.VMEM((2, G, SPAN), BF16),
            pltpu.VMEM((G, WA), BF16),
            pltpu.VMEM((NZ, G, WB), BF16),
            pltpu.VMEM((NZ, G, WA), BF16),
            pltpu.VMEM((NZ, G, WB), BF16),
            pltpu.VMEM((2, TOK), jnp.int32),
            pltpu.VMEM((2, TOK), jnp.int32),
            pltpu.VMEM((DIN, SPAN), BF16),
            pltpu.VMEM((NY, SPAN, DIN), BF16),
            pltpu.VMEM((NY, SPAN, DOUT), BF16),
            pltpu.VMEM((2, ROWS, HALF), BF16),
            pltpu.VMEM((2, ROWS, HALF), BF16),
            pltpu.VMEM((NZ, NY, G, QX), F32),
            pltpu.VMEM((2, 4, NY, G, QX), BF16),
            pltpu.VMEM((2, 4, NY, G, QX), BF16),
            pltpu.VMEM((3, SPAN, 1024), F32),
            pltpu.VMEM((3, SPAN, 1024), BF16),
            pltpu.VMEM((2, 3, SPAN, 1024), F32),
            pltpu.VMEM((3, SPAN, 1024), BF16),
            pltpu.VMEM((2, 3, SPAN, 1024), BF16),
            pltpu.VMEM((2, 3, SPAN, 1024), BF16),
            pltpu.VMEM((NY, G, QX), BF16),
            pltpu.VMEM((NY, 2, G, QX), BF16),
            pltpu.VMEM((NC, QT, QX), F32),
            pltpu.VMEM((NY, QT, QX), BF16),
            pltpu.VMEM((TOK, QX), BF16),
            pltpu.VMEM((DIN, SPAN), BF16),
            pltpu.VMEM((SPAN, DOUT), BF16),
            dma((7,)),
            dma((4,)),
            *pair(2, 4), *pair(2, 4), *pair(8), *pair(8), *pair(1),
            *pair(8, 3), *pair(3), *pair(2, 4, NX), *pair(3, 2), *pair(2, 4, NY), *pair(2, 3), *pair(2, 3),
            *pair(E - 1, NY), *pair(3),
        ],
        compiler_params=pltpu.CompilerParams(
            collective_id=0, has_side_effects=True, vmem_limit_bytes=60 * 1024 * 1024
        ),
        cost_estimate=pl.CostEstimate(flops=11_300_000_000, bytes_accessed=5_000_000, transcendentals=0),
        name="moe_backward",
    )(features, cotangent, expert_ids.T, gate_levels.T, w_in, w_out)
    return pl.pallas_call(
        hand_over,
        out_shape=tuple(jax.ShapeDtypeStruct(g.shape, g.dtype) for g in grads),
        in_specs=[hbm] * 3,
        out_specs=(hbm,) * 3,
        scratch_shapes=[*(pltpu.VMEM(g.shape, g.dtype) for g in grads), dma((2, 3))],
        name="hand_over",
    )(*grads)


def solution(mesh):
    return jax.shard_map(
        shards,
        mesh=mesh,
        in_specs=(
            P("ep", None),
            P("ep", None),
            P("ep", None),
            P("ep", None),
            P("ep", None, "tp"),
            P("ep", "tp", None),
        ),
        out_specs=(P("ep", "tp"), P("ep", None, "tp"), P("ep", "tp", None)),
        check_vma=False,
    )
```

```python
import functools
import math

import jax
import jax.numpy as jnp
from jax import lax
from jax.experimental import pallas as pl
from jax.experimental.pallas import tpu as pltpu
from jax.sharding import PartitionSpec as P

MESH = pl.DeviceIdType.MESH
E = 8
NZ, NX, NC, NY = 8, 4, 2, 4
TOK = 256
QT = TOK // NY
DIN = 1024
DOUT = 2048
SPAN = 128
QX = DIN // NY
SL = 48
RB = 32
G = NX * SL
CB = 512
WB = DIN + CB
WA = DOUT - CB
HALF = 2 * SPAN
ROWS = NZ * G
F32 = jnp.float32
BF16 = jnp.bfloat16


def dot_nn(a, b):
    return lax.dot_general(a, b, (((1,), (0,)), ((), ())), preferred_element_type=F32)


def dot_nt(a, b):
    return lax.dot_general(a, b, (((1,), (1,)), ((), ())), preferred_element_type=F32)


def dot_tn(a, b):
    return lax.dot_general(a, b, (((0,), (0,)), ((), ())), preferred_element_type=F32)


def gelu_parts(v):
    k = math.sqrt(2.0 / math.pi)
    vv = v * v
    t = jnp.tanh(k * (v + 0.044715 * (v * vv)))
    half = 0.5 * (1.0 + t)
    act = v * half
    slope = half + 0.5 * v * (1.0 - t * t) * (k * (1.0 + 3.0 * 0.044715 * vv))
    return act, slope


def kernel(
    grad_scale,
    x_ref, dy_ref, ids_hbm, gate_hbm, w1_ref, w2_ref,
    gin_ref, g1_ref, g2_ref,
    rawb, rawa, meta, p_ref, pg_ref, p_all, packa, packb, rowsa, rowsb,
    ids_ref, gate_ref, w1v, w1b, w2b, actb, bpb, pown, sbuf, rbuf, gown, gfar, gnear, ghalf, gsend, grecv,
    retb, retr, tokens, giny, gout,
    ld, zb_s, zb_r, zm_s, zm_r, sb_s, sb_r, sm_s, sm_r, sa_s, sa_r,
    xb_s, xb_r, xa_s, xa_r, za_s, za_r, wy_s, wy_r, rs_s, rs_r, gh_s, gh_r, gy_s, gy_r,
    rt_s, rt_r, yo_s, yo_r,
):
    ep = lax.axis_index("ep")
    y = lax.axis_index("tp")
    z = ep // E
    me = lax.rem(ep, E)
    x = me // NC
    c = lax.rem(me, NC)
    right = (lax.rem(z + 1, NZ) * E + me, y)
    left = (lax.rem(z + NZ - 1, NZ) * E + me, y)
    sibling = (z * E + me + 1 - 2 * c, y)

    def xrank(k):
        return lax.rem(x + k, NX)

    def xdev(k):
        return (z * E + xrank(k) * NC + c, y)

    def yrank(k):
        return lax.rem(y + k, NY)

    def plane(m):
        return (z * E + lax.rem(me + m, E), y)

    def remote(src, dst, ss, rs, dev):
        return pltpu.make_async_remote_copy(
            src_ref=src, dst_ref=dst, send_sem=ss, recv_sem=rs, device_id=dev, device_id_type=MESH
        )

    quarter = pl.ds(pl.multiple_of(y * QT, QT), QT)
    loads = [
        pltpu.make_async_copy(x_ref.at[quarter], rawb.at[0, c, :, pl.ds(0, DIN)], ld.at[0]),
        pltpu.make_async_copy(dy_ref.at[quarter, pl.ds(0, CB)], rawb.at[0, c, :, pl.ds(DIN, CB)], ld.at[1]),
        pltpu.make_async_copy(dy_ref.at[quarter, pl.ds(CB, WA)], rawa.at[c], ld.at[2]),
        pltpu.make_async_copy(w2_ref.at[0], w2b.at[0], ld.at[3]),
        pltpu.make_async_copy(w1_ref.at[0], w1v, ld.at[4]),
        pltpu.make_async_copy(ids_hbm, ids_ref, ld.at[5]),
        pltpu.make_async_copy(gate_hbm, gate_ref, ld.at[6]),
    ]
    for load in loads:
        load.start()

    bar = pltpu.get_barrier_semaphore()
    partners = [left, right]
    partners += [plane(m) for m in range(1, E)] + [(ep, yrank(k)) for k in range(1, NY)]
    for dev in partners:
        pl.semaphore_signal(bar, inc=1, device_id=dev, device_id_type=MESH)
    pl.semaphore_wait(bar, len(partners))

    def slots(direction, step):
        src = 0 if step == 0 else 2 * step - 1 + direction
        return src, (7 if step == 3 else 2 * step + 1 + direction)

    def toward(direction):
        return left if direction == 0 else right

    def raw_ring(direction, step):
        s, d = slots(direction, step)
        src, dst = rawb.at[s, c], rawb.at[d, c]
        if step == 3:
            half = pl.ds(direction * (QT // 2), QT // 2)
            src, dst = src.at[half], dst.at[half]
        return remote(src, dst, zb_s.at[direction, step], zb_r.at[direction, step], toward(direction))

    def meta_ring(direction, step):
        s, d = slots(direction, step)
        return remote(meta.at[s, c], meta.at[d, c], zm_s.at[direction, step], zm_r.at[direction, step],
                      toward(direction))

    def has_meta(direction, step):
        return step < 3 or direction == 0

    def row_ring(direction, step, k):
        s, d = slots(direction, step)
        piece = pl.ds(pl.multiple_of(xrank(k) * SL, 16), SL)
        return remote(rowsa.at[s, piece], rowsa.at[d, piece], za_s.at[direction, step, k], za_r.at[direction, step, k],
                      toward(direction))

    def row_pieces(direction, step):
        if step == 3:
            return (0, 2) if direction == 0 else (1, 3)
        return (0, 1, 3, 2)

    def raw_sib(slot, core):
        return remote(rawb.at[slot, core], rawb.at[slot, core], sb_s.at[slot], sb_r.at[slot], sibling)

    def meta_sib(slot, core):
        return remote(meta.at[slot, core], meta.at[slot, core], sm_s.at[slot], sm_r.at[slot], sibling)

    def cot_sib(core):
        return remote(rawa.at[core], rawa.at[core], sa_s.at[0], sa_r.at[0], sibling)

    loads[2].wait()
    cot_sib(c).start()
    loads[0].wait()
    loads[1].wait()
    raw_sib(0, c).start()
    for direction in range(2):
        raw_ring(direction, 0).start()

    loads[5].wait()
    loads[6].wait()
    expert = lax.broadcasted_iota(jnp.int32, (16, TOK), 0)
    first = jnp.broadcast_to(ids_ref[0:1], (16, TOK)) == expert
    second = jnp.broadcast_to(ids_ref[1:2], (16, TOK)) == expert
    gates = gate_ref[...].astype(F32) * (1.0 / 16.0)
    named = jnp.where(first | second, 1.0, 0.0)
    gate_of = jnp.where(first, jnp.broadcast_to(gates[0:1], (16, TOK)), 0.0) + jnp.where(
        second, jnp.broadcast_to(gates[1:2], (16, TOK)), 0.0)
    token = lax.broadcasted_iota(jnp.int32, (TOK, SPAN), 0)
    place = lax.broadcasted_iota(jnp.int32, (TOK, SPAN), 1)
    taken = (token - place == QT * (y - c)) & (place >= QT * c) & (place < QT * c + QT)
    pick = jnp.where(taken, 1.0, 0.0).astype(BF16)
    named_q = dot_nn(named.astype(BF16), pick)
    gate_q = dot_nn(gate_of.astype(BF16), pick)
    earlier = jnp.where(
        lax.broadcasted_iota(jnp.int32, (SPAN, SPAN), 0) < lax.broadcasted_iota(jnp.int32, (SPAN, SPAN), 1), 1.0, 0.0
    ).astype(BF16)
    rank = dot_nn(named_q.astype(BF16), earlier)
    base = jnp.where(c == 0, 1.0, 1.0 + SL // NC)
    meta[0, c, 0:16] = jnp.where(named_q > 0.5, rank + base, 0.0).astype(BF16)
    meta[0, c, 16:32] = gate_q.astype(BF16)
    meta_sib(0, c).start()
    for direction in range(2):
        meta_ring(direction, 0).start()

    def w2_send(j):
        return remote(w2b.at[0], w2b.at[NY - j], wy_s.at[j - 1, 1], wy_r.at[NY - j - 1, 1], (ep, yrank(j)))

    def w1_send(j):
        return remote(w1b.at[0], w1b.at[NY - j], wy_s.at[j - 1, 0], wy_r.at[NY - j - 1, 0], (ep, yrank(j)))

    def w2_recv(j):
        return remote(w2b.at[0], w2b.at[j], wy_s.at[j - 1, 1], wy_r.at[j - 1, 1], (ep, yrank(j)))

    def w1_recv(j):
        return remote(w1b.at[0], w1b.at[j], wy_s.at[j - 1, 0], wy_r.at[j - 1, 0], (ep, yrank(j)))

    loads[3].wait()
    for j in (2, 1, 3):
        w2_send(j).start()

    def build(slot):
        both = meta[slot, 0].astype(F32) + meta[slot, 1].astype(F32)
        want = lax.broadcasted_iota(jnp.int32, (SL, SPAN), 0).astype(F32) + 1.0
        for k in range(NX):
            row = jnp.where(c == 0, both[2 * k:2 * k + 1], both[2 * k + 1:2 * k + 2])
            gate = jnp.where(c == 0, both[16 + 2 * k:17 + 2 * k], both[17 + 2 * k:18 + 2 * k])
            hit = jnp.broadcast_to(row, (SL, SPAN)) == want
            chosen = jnp.where(hit, 1.0, 0.0).astype(BF16)
            p_ref[slot, k * SL:(k + 1) * SL] = chosen
            if slot == 0:
                back = lax.broadcasted_iota(jnp.int32, (RB, SPAN), 0).astype(F32) + jnp.where(c == 0, 1.0, 17.0)
                swap = jnp.where(c == 0, both[2 * k + 1:2 * k + 2], both[2 * k:2 * k + 1])
                for i, line in enumerate((row, swap)):
                    p_all[i, k * RB:(k + 1) * RB] = jnp.where(
                        jnp.broadcast_to(line, (RB, SPAN)) == back, 1.0, 0.0).astype(BF16)
            pg_ref[slot, k * SL:(k + 1) * SL] = jnp.where(
                hit, jnp.broadcast_to(gate, (SL, SPAN)), 0.0).astype(BF16)

    def xrows(k):
        return pl.ds(pl.multiple_of(k * SL, 16), SL)

    def packb_send(slot, k):
        return remote(packb.at[slot, xrows(xrank(k))], rowsb.at[slot, xrows(x)], xb_s.at[slot, k - 1],
                      xb_r.at[slot, k - 1], xdev(k))

    def packb_recv(slot, k):
        return remote(packb.at[slot, xrows(xrank(k))], rowsb.at[slot, xrows(xrank(NX - k))], xb_s.at[slot, k - 1],
                      xb_r.at[slot, k - 1], xdev(k))

    def packa_send(k):
        return remote(packa.at[xrows(xrank(k))], rowsa.at[0, xrows(x)], xa_s.at[k - 1], xa_r.at[k - 1], xdev(k))

    def packa_recv(k):
        return remote(packa.at[xrows(xrank(k))], rowsa.at[0, xrows(xrank(NX - k))], xa_s.at[k - 1], xa_r.at[k - 1],
                      xdev(k))

    def pack_b(slot):
        packb[slot, :, 0:DIN] = dot_nn(p_ref[slot], rawb[slot, :, :, 0:DIN].reshape(SPAN, DIN)).astype(BF16)
        packb[slot, :, DIN:WB] = dot_nn(pg_ref[slot], rawb[slot, :, :, DIN:WB].reshape(SPAN, CB)).astype(BF16)

    def send_b(slot):
        for k in (2, 1, 3):
            packb_send(slot, k).start()
        rowsb[slot, xrows(x)] = packb[slot, xrows(x)]

    meta_sib(0, 1 - c).wait_recv()
    build(0)
    cot_sib(1 - c).wait_recv()
    packa[...] = dot_nn(pg_ref[0], rawa[...].reshape(SPAN, WA)).astype(BF16)
    for k in (1, 3, 2):
        packa_send(k).start()
    rowsa[0, xrows(x)] = packa[xrows(x)]

    def raw_pass(step):
        for direction in range(2):
            raw_ring(direction, step - 1).wait_recv()
            if step <= 3:
                raw_ring(direction, step).start()
            if has_meta(direction, step - 1):
                meta_ring(direction, step - 1).wait_recv()
                if step <= 3 and has_meta(direction, step):
                    meta_ring(direction, step).start()
            if step <= 3:
                slot = slots(direction, step - 1)[1]
                raw_sib(slot, c).start()
                meta_sib(slot, c).start()
        if step == 4:
            raw_sib(7, c).start()
            meta_sib(7, c).start()

    def sib_pass(slot):
        raw_sib(slot, 1 - c).wait_recv()
        meta_sib(slot, 1 - c).wait_recv()
        build(slot)
        pack_b(slot)

    def row_start(k):
        for direction in range(2):
            row_ring(direction, 0, k).start()

    def row_pass(step, k):
        for direction in range(2):
            if k in row_pieces(direction, step - 1):
                row_ring(direction, step - 1, k).wait_recv()
                if step <= 3 and k in row_pieces(direction, step):
                    row_ring(direction, step, k).start()

    row_start(0)
    raw_pass(1)
    raw_sib(0, 1 - c).wait_recv()
    pack_b(0)
    packa_recv(3).wait_recv()
    row_start(1)
    packa_recv(1).wait_recv()
    row_start(3)
    send_b(0)
    sib_pass(1)
    sib_pass(2)
    send_b(1)
    send_b(2)
    packa_recv(2).wait_recv()
    row_start(2)
    raw_pass(2)
    loads[4].wait()
    w1b[0] = w1v[...].astype(F32).T.astype(BF16)
    for j in (2, 1, 3):
        w1_send(j).start()
    sib_pass(3)
    sib_pass(4)
    send_b(3)
    send_b(4)
    row_pass(1, 0)
    raw_pass(3)
    row_pass(1, 1)
    sib_pass(5)
    sib_pass(6)
    send_b(5)
    send_b(6)
    row_pass(1, 3)
    raw_pass(4)
    row_pass(1, 2)
    sib_pass(7)
    send_b(7)
    row_pass(2, 0)
    row_pass(2, 1)

    def forward(s0, n):
        for slot in range(s0, s0 + n):
            for k in (1, 3, 2):
                packb_recv(slot, k).wait_recv()
        rows = slice(s0 * G, (s0 + n) * G)

        @pl.loop(0, 2)
        def _(h):
            w1 = w1b[pl.ds(2 * h, 2)].reshape(HALF, DIN)
            w2 = w2b[pl.ds(2 * h, 2)].reshape(HALF, DOUT)
            pre = dot_nt(rowsb[s0:s0 + n, :, 0:DIN].reshape(n * G, DIN), w1)
            back = dot_nt(rowsb[s0:s0 + n, :, DIN:WB].reshape(n * G, CB), w2[:, 0:CB])
            back += dot_nt(rowsa[s0:s0 + n].reshape(n * G, WA), w2[:, CB:DOUT])
            act, slope = gelu_parts(pre)
            actb[h, rows] = act.astype(BF16)
            bpb[h, rows] = (back * slope).astype(BF16)

        for q in range(NY):
            cols = slice(q * QX, (q + 1) * QX)
            part = dot_nn(bpb[0, rows], w1b[0:2, :, cols].reshape(HALF, QX))
            part += dot_nn(bpb[1, rows], w1b[2:4, :, cols].reshape(HALF, QX))
            pown[s0:s0 + n, q] = part.reshape(n, G, QX)

    for j in (1, 3, 2):
        w2_recv(j).wait_recv()
        w1_recv(j).wait_recv()
    forward(0, 1)
    row_pass(2, 3)
    row_pass(2, 2)
    row_pass(3, 0)
    forward(1, 2)
    row_pass(3, 1)
    row_pass(3, 3)
    row_pass(3, 2)
    forward(3, 2)
    forward(5, 2)
    for k in range(NX):
        row_pass(4, k)
    forward(7, 1)

    def rs(direction, step, ch):
        src, dst = sbuf.at[direction, step, ch], rbuf.at[direction, step, ch]
        if step == 0:
            half = pl.ds(direction * (G // 2), G // 2)
            src, dst = src.at[half], dst.at[half]
        return remote(src, dst, rs_s.at[direction, step, ch], rs_r.at[direction, step, ch],
                      right if direction == 0 else left)

    turns = [yrank(j) for j in (2, 1, 3, 0)]
    for ch in turns:
        for direction in range(2):
            half = slice(direction * (G // 2), (direction + 1) * (G // 2))
            sbuf[direction, 0, ch, half] = pown[7, ch, half].astype(BF16)
            rs(direction, 0, ch).start()

    def rs_pass(step, ch):
        for direction in range(2):
            slot = 7 - 2 * step + direction
            rs(direction, step - 1, ch).wait_recv()
            if step == 1:
                got = slice(direction * (G // 2), (direction + 1) * (G // 2))
                rest = slice((1 - direction) * (G // 2), (2 - direction) * (G // 2))
                sbuf[direction, step, ch, rest] = pown[slot, ch, rest].astype(BF16)
            else:
                got = slice(0, G)
            sbuf[direction, step, ch, got] = (
                pown[slot, ch, got] + rbuf[direction, step - 1, ch, got].astype(F32)
            ).astype(BF16)
            rs(direction, step, ch).start()

    ways = (1, NY - 1)

    def half_rows(way):
        return pl.ds(way * (SPAN // 2), SPAN // 2)

    def grad_half(way, ch):
        return remote(gfar.at[ch, half_rows(way)], ghalf.at[ch, half_rows(way)], gh_s.at[way, ch], gh_r.at[way, ch],
                      (ep, yrank(ways[way])))

    def grad_send(way, ch):
        return remote(gsend.at[way, ch], grecv.at[way, ch], gy_s.at[way, ch], gy_r.at[way, ch], (ep, yrank(ways[way])))

    def grad_near(way, ch):
        grad_half(way, ch).wait_recv()
        got = half_rows(way)
        rest = half_rows(1 - way)
        gsend[way, ch, rest] = gnear[way, ch, rest].astype(BF16)
        gsend[way, ch, got] = (gnear[way, ch, got] + ghalf[ch, got].astype(F32)).astype(BF16)
        grad_send(way, ch).start()

    def weight_grads(h, ch):
        left_side = bpb[h] if ch == 0 else actb[h]
        for part in range(2):
            col = part * 512
            if ch == 0:
                right_side = rowsb[:, :, col:col + 512]
            elif ch == 1 and part == 0:
                right_side = rowsb[:, :, DIN:WB]
            else:
                at = (ch - 1) * 1024 + col - CB
                right_side = rowsa[:, :, at:at + 512]
            total = dot_tn(left_side, right_side.reshape(ROWS, 512))
            for i in range(2):
                j = 2 * h + i
                block = total[i * SPAN:(i + 1) * SPAN]
                if j == 0:
                    gown[ch, :, col:col + 512] = block
                elif j == 2:
                    gfar[ch, :, col:col + 512] = block.astype(BF16)
                else:
                    gnear[j // 2, ch, :, col:col + 512] = block
        for way in range(2):
            if h == 1:
                grad_half(way, ch).start()
            else:
                grad_near(way, ch)

    weight_grads(1, 1)
    rs_pass(1, turns[0])
    weight_grads(1, 2)
    rs_pass(1, turns[1])
    rs_pass(1, turns[2])
    weight_grads(1, 0)
    rs_pass(1, turns[3])
    weight_grads(0, 1)
    rs_pass(2, turns[0])
    weight_grads(0, 2)
    rs_pass(2, turns[1])
    weight_grads(0, 0)
    rs_pass(2, turns[2])
    rs_pass(2, turns[3])
    for ch in turns:
        rs_pass(3, ch)

    def rows_for(chip, core):
        return pl.ds(pl.multiple_of(chip * SL + core * (SL - RB), 16), RB)

    def rows_from(chip):
        return pl.ds(pl.multiple_of(chip * RB, RB), RB)

    def ret_send(m, ch):
        to = lax.rem(me + m, E)
        return remote(retb.at[ch, rows_for(to // NC, lax.rem(to, NC))], retr.at[ch, m % 2, rows_from(x)],
                      rt_s.at[m - 1, ch], rt_r.at[m - 1, ch], plane(m))

    def ret_recv(m, ch):
        source = lax.rem(me + E - m, E)
        return remote(retb.at[ch, rows_for(x, c)], retr.at[ch, m % 2, rows_from(source // NC)],
                      rt_s.at[m - 1, ch], rt_r.at[m - 1, ch], plane(m))

    def out_send(j):
        return remote(giny.at[yrank(j)], gout.at[quarter], yo_s.at[j - 1], yo_r.at[j - 1], (ep, yrank(j)))

    def out_recv(j):
        return remote(giny.at[yrank(j)], gout.at[pl.ds(pl.multiple_of(yrank(NY - j) * QT, QT), QT)], yo_s.at[j - 1],
                      yo_r.at[j - 1], (ep, yrank(j)))

    far_first = (4, 3, 5, 2, 6, 1, 7)

    def tail_rows(j):
        ch = yrank(j)
        for direction in range(2):
            rs(direction, 3, ch).wait_recv()
        retb[ch] = (pown[0, ch] + rbuf[0, 3, ch].astype(F32) + rbuf[1, 3, ch].astype(F32)).astype(BF16)
        for m in far_first:
            ret_send(m, ch).start()
        retr[ch, 0, rows_from(x)] = retb[ch, rows_for(x, c)]

    def tail_tokens(j):
        ch = yrank(j)
        for m in far_first:
            ret_recv(m, ch).wait_recv()
        tokens[...] = dot_tn(p_all[...].reshape(2 * NX * RB, SPAN), retr[ch].reshape(2 * NX * RB, QX)).reshape(NC, QT, QX)
        if j:
            giny[ch] = tokens[c].astype(BF16)
            out_send(j).start()
        else:
            gout[quarter] = tokens[c].astype(BF16)

    def finish(ch):
        for way in range(2):
            grad_send(way, ch).wait_recv()
        total = (gown[ch] + grecv[0, ch].astype(F32) + grecv[1, ch].astype(F32)) * grad_scale
        if ch == 0:
            g1_ref[0] = total.T.astype(BF16)
        else:
            g2_ref[0, :, (ch - 1) * 1024:ch * 1024] = total.astype(BF16)

    finish(1)
    tail_rows(2)
    finish(2)
    tail_rows(1)
    tail_tokens(2)
    finish(0)
    tail_rows(3)
    tail_tokens(1)
    tail_rows(0)
    tail_tokens(3)
    tail_tokens(0)
    for j in (1, 3, 2):
        out_recv(j).wait_recv()
    gin_ref[...] = gout[...]

    for direction in range(2):
        for step in range(4):
            raw_ring(direction, step).wait_send()
            if has_meta(direction, step):
                meta_ring(direction, step).wait_send()
            for k in row_pieces(direction, step):
                row_ring(direction, step, k).wait_send()
            for ch in range(NY):
                rs(direction, step, ch).wait_send()
    for slot in range(8):
        raw_sib(slot, c).wait_send()
        meta_sib(slot, c).wait_send()
        for k in range(1, NX):
            packb_send(slot, k).wait_send()
    cot_sib(c).wait_send()
    for k in range(1, NX):
        packa_send(k).wait_send()
    for m in range(1, E):
        for ch in range(NY):
            ret_send(m, ch).wait_send()
    for j in range(1, NY):
        w1_send(j).wait_send()
        w2_send(j).wait_send()
        out_send(j).wait_send()
    for way in range(2):
        for ch in range(3):
            grad_half(way, ch).wait_send()
            grad_send(way, ch).wait_send()


def hand_over(a_ref, b_ref, c_ref, a_out, b_out, c_out, sems):
    copies = [
        pltpu.make_async_copy(src, dst, sems.at[i])
        for i, (src, dst) in enumerate(((a_ref, a_out), (b_ref, b_out), (c_ref, c_out)))
    ]
    for copy in copies:
        copy.start()
    for copy in copies:
        copy.wait()


def shards(features, cotangent, expert_ids, gate_levels, w_in, w_out):
    tokens = features.shape[0] * lax.axis_size("ep")
    grad_scale = 1.0 / math.sqrt(2.0 * tokens / E)
    hbm = pl.BlockSpec(memory_space=pl.ANY)
    vmem = pl.BlockSpec(memory_space=pltpu.VMEM)
    dma = pltpu.SemaphoreType.DMA

    def pair(*shape):
        return [dma(shape), dma(shape)]

    grads = pl.pallas_call(
        functools.partial(kernel, grad_scale),
        out_shape=(
            pltpu.VMEM((TOK, QX), BF16),
            pltpu.VMEM((1, DIN, SPAN), BF16),
            pltpu.VMEM((1, SPAN, DOUT), BF16),
        ),
        in_specs=[hbm] * 6,
        out_specs=(vmem,) * 3,
        scratch_shapes=[
            pltpu.VMEM((NZ, NC, QT, WB), BF16),
            pltpu.VMEM((NC, QT, WA), BF16),
            pltpu.VMEM((NZ, NC, 32, SPAN), BF16),
            pltpu.VMEM((NZ, G, SPAN), BF16),
            pltpu.VMEM((NZ, G, SPAN), BF16),
            pltpu.VMEM((2, NX * RB, SPAN), BF16),
            pltpu.VMEM((G, WA), BF16),
            pltpu.VMEM((NZ, G, WB), BF16),
            pltpu.VMEM((NZ, G, WA), BF16),
            pltpu.VMEM((NZ, G, WB), BF16),
            pltpu.VMEM((2, TOK), jnp.int32),
            pltpu.VMEM((2, TOK), jnp.int32),
            pltpu.VMEM((DIN, SPAN), BF16),
            pltpu.VMEM((NY, SPAN, DIN), BF16),
            pltpu.VMEM((NY, SPAN, DOUT), BF16),
            pltpu.VMEM((2, ROWS, HALF), BF16),
            pltpu.VMEM((2, ROWS, HALF), BF16),
            pltpu.VMEM((NZ, NY, G, QX), F32),
            pltpu.VMEM((2, 4, NY, G, QX), BF16),
            pltpu.VMEM((2, 4, NY, G, QX), BF16),
            pltpu.VMEM((3, SPAN, 1024), F32),
            pltpu.VMEM((3, SPAN, 1024), BF16),
            pltpu.VMEM((2, 3, SPAN, 1024), F32),
            pltpu.VMEM((3, SPAN, 1024), BF16),
            pltpu.VMEM((2, 3, SPAN, 1024), BF16),
            pltpu.VMEM((2, 3, SPAN, 1024), BF16),
            pltpu.VMEM((NY, G, QX), BF16),
            pltpu.VMEM((NY, 2, NX * RB, QX), BF16),
            pltpu.VMEM((NC, QT, QX), F32),
            pltpu.VMEM((NY, QT, QX), BF16),
            pltpu.VMEM((TOK, QX), BF16),
            dma((7,)),
            *pair(2, 4), *pair(2, 4), *pair(8), *pair(8), *pair(1),
            *pair(8, 3), *pair(3), *pair(2, 4, NX), *pair(3, 2), *pair(2, 4, NY), *pair(2, 3), *pair(2, 3),
            *pair(E - 1, NY), *pair(3),
        ],
        compiler_params=pltpu.CompilerParams(
            collective_id=0, has_side_effects=True, vmem_limit_bytes=60 * 1024 * 1024
        ),
        cost_estimate=pl.CostEstimate(flops=11_300_000_000, bytes_accessed=5_000_000, transcendentals=0),
        name="moe_backward",
    )(features, cotangent, expert_ids.T, gate_levels.T, w_in, w_out)
    return pl.pallas_call(
        hand_over,
        out_shape=tuple(jax.ShapeDtypeStruct(g.shape, g.dtype) for g in grads),
        in_specs=[vmem] * 3,
        out_specs=(hbm,) * 3,
        scratch_shapes=[dma((3,))],
        name="hand_over",
    )(*(pltpu.with_memory_space_constraint(g, pltpu.VMEM) for g in grads))


def solution(mesh):
    return jax.shard_map(
        shards,
        mesh=mesh,
        in_specs=(
            P("ep", None),
            P("ep", None),
            P("ep", None),
            P("ep", None),
            P("ep", None, "tp"),
            P("ep", "tp", None),
        ),
        out_specs=(P("ep", "tp"), P("ep", None, "tp"), P("ep", "tp", None)),
        check_vma=False,
    )
```
